128 devices in a mesh: gx: 4 (over z), gz: 16 (over y, x_hi, core), sa: 2 (over x_lo).
Axes of the slice: x: 4 (x_hi: 2, x_lo: 2; x = x_hi * 2 + x_lo), y: 4, z: 4, core: 2. Of those that a mesh axis runs over, the one named last changes fastest.
Arguments:
- forcing: float32 [3, 8, 128, 128, 256], P(None, 'sa', 'gx', 'gz'), may hold values from -60 to 60
- velocity: float32 [256], replicated, may hold values from 0.3 to 1.2
- wall_solve: float32 [256, 256], replicated, may hold values from -1 to 1.7
Outputs:
- basis: float32 [3, 8, 128, 128, 256], P(None, 'sa', 'gx', 'gz')
- factor: float32 [8, 8], replicated
The draws below stay inside these ranges and needn't reach their ends.
All inputs are finite; a program needn't handle non-finite values.
Results may differ from the reference program's by a relative error of at most 0.00015.
Values sent between devices are 32-bit elements; how exact they have to be, the bound alone decides.
A program may use at most 64 MiB of HBM per device.

```python
import math
import jax
import jax.numpy as jnp
from jax import lax

NY = 256
NX = 128
NZ = 128
SKETCH = 8


def draw_forcing(key, part):
    noise_key = jax.random.fold_in(key, 11)
    mixing_key = jax.random.fold_in(key, 13)
    shared_key = jax.random.fold_in(key, 14)
    place_x = jnp.arange(NX, dtype=jnp.float32) / NX
    place_z = jnp.arange(NZ, dtype=jnp.float32) / NZ
    shape = (3, SKETCH + 1, NX, NZ, NY)
    noise = jnp.clip(jax.random.normal(noise_key, shape, jnp.float32), -6.0, 6.0)
    envelope = jnp.exp(0.55 * (place_x[:, None] + place_z[None, :]))
    fields = noise * envelope[:, :, None]
    spread = 0.8 / (SKETCH - 1)
    unit_matrix = jnp.eye(SKETCH, dtype=jnp.float32)
    off_terms = jax.random.uniform(mixing_key, (SKETCH, SKETCH), jnp.float32, -spread, spread) * (1.0 - unit_matrix)
    mixing = unit_matrix + off_terms
    shared_weight = jax.random.uniform(shared_key, (SKETCH,), jnp.float32, 0.5, 0.9)
    value = shared_weight[None, :, None, None, None] * fields[:, SKETCH:SKETCH + 1]
    for source in range(SKETCH):
        value = value + mixing[:, source][None, :, None, None, None] * fields[:, source:source + 1]
    return value / 2.7


def draw_wall_solve(key, part):
    first_key, second_key = jax.random.split(key)
    diagonal = 1.0 + 0.3 * jax.random.uniform(first_key, (NY,), jnp.float32)
    spread = jnp.clip(jax.random.normal(second_key, (NY, NY), jnp.float32), -4.0, 4.0)
    return jnp.diag(diagonal) + spread * (0.5 / math.sqrt(NY))


def setup_inputs(seed: int = 0) -> dict:
    keys = jax.random.split(jax.random.key(seed), 4)
    return {
        "forcing": draw_forcing(jax.random.fold_in(keys[3], 71), 0),
        "velocity": jnp.clip(jnp.exp(jax.random.uniform(keys[1], (NY,), jnp.float32, math.log(0.3), math.log(1.2))), 0.3, 1.2),
        "wall_solve": draw_wall_solve(jax.random.fold_in(keys[3], 71), 0),
    }


step_length = 0.4
viscosity = 0.2

def shear_of(velocity):
    inner = (velocity[2:] - velocity[:-2]) * 0.5
    return jnp.concatenate([velocity[1:2] - velocity[0:1], inner, velocity[-1:] - velocity[-2:-1]])

def upper_factor(gram):
    order_size = gram.shape[0]
    column_ids = jnp.arange(order_size)
    row_list = []
    for pivot_index in range(order_size):
        current_row = gram[pivot_index]
        for other_index in range(pivot_index):
            current_row = current_row - row_list[other_index][pivot_index] * row_list[other_index]
        current_row = jnp.where(column_ids >= pivot_index, current_row, jnp.zeros_like(current_row)) / jnp.sqrt(current_row[pivot_index])
        row_list.append(current_row)
    return jnp.stack(row_list)

def upper_inverse(factor):
    order_size = factor.shape[0]
    identity_rows = jnp.eye(order_size, dtype=factor.dtype)
    row_list = [None] * order_size
    for pivot_index in range(order_size - 1, -1, -1):
        current_row = identity_rows[pivot_index]
        for other_index in range(pivot_index + 1, order_size):
            current_row = current_row - factor[pivot_index, other_index] * row_list[other_index]
        row_list[pivot_index] = current_row / factor[pivot_index, pivot_index]
    return jnp.stack(row_list)

def operate(field, velocity, shear_rate, adjoint):
    east_side = jnp.roll(field, -1, axis=2)
    west_side = jnp.roll(field, 1, axis=2)
    north_side = jnp.roll(field, -1, axis=3)
    south_side = jnp.roll(field, 1, axis=3)
    direction = 1.0 if adjoint else -1.0
    change = direction * velocity * (east_side - west_side) * 0.5 + viscosity * (east_side + west_side + north_side + south_side - 4.0 * field)
    if adjoint:
        return change.at[1].add(-shear_rate * field[0])
    return change.at[0].add(-shear_rate * field[1])

def reference(forcing, velocity, wall_solve):
    shear_rate = shear_of(velocity)
    current = forcing
    for repeat in range(2):
        current = jnp.matmul(current + step_length * (operate(current, velocity, shear_rate, False) + forcing), wall_solve, precision=lax.Precision.HIGHEST)
    entries = 3 * NX * NZ * NY
    partial_value = lax.optimization_barrier(jnp.sum(current * current, axis=(0, 2, 3, 4)))
    scales = jnp.sqrt(partial_value / entries + 1e-06)
    response = current / scales[None, :, None, None, None]
    current = response
    for repeat in range(2):
        solved = jnp.matmul(current, wall_solve.T, precision=lax.Precision.HIGHEST)
        current = solved + step_length * operate(solved, velocity, shear_rate, True) + step_length * response
    gram = jnp.einsum('cixzy,cjxzy->ij', current, current, precision=lax.Precision.HIGHEST) / entries
    factor = upper_factor(gram)
    inverse = upper_inverse(factor)
    basis = jnp.einsum('cixzy,ij->cjxzy', current, inverse, precision=lax.Precision.HIGHEST)
    return (basis, factor)
```

```python
import functools

import jax
import jax.numpy as jnp
from jax import lax
from jax.experimental import pallas as pl
from jax.experimental.pallas import tpu as pltpu
from jax.sharding import PartitionSpec as P

MESH = pl.DeviceIdType.MESH
step_length = 0.4
viscosity = 0.2
GROUPS = ((2, 1, 16), (0, 2, 8))
BLOCKS = 4
CELLS = 32
NY = 256
ROWS = 512


def kernel(
    entries,
    forcing,
    velocity,
    wall,
    basis,
    factor_out,
    field0,
    field1,
    field2,
    field3,
    held,
    sketch,
    other,
    edge_out,
    edge_in,
    lhs,
    solve,
    solve_t,
    drift_row,
    shear_row,
    squares,
    local_gram,
    row_sums,
    y_sums,
    z_sums,
    splats,
    coefs,
    load_sem,
    send_sem,
    recv_sem,
    sketch_send,
    sketch_recv,
    sum_send,
    sum_recv,
    store_sem,
):
    gx, gz, sa = lax.axis_index("gx"), lax.axis_index("gz"), lax.axis_index("sa")
    in_row, y = lax.rem(gz, 4), lax.div(gz, 4)
    rank = in_row * 2 + sa

    def row_peer(offset):
        other_rank = lax.rem(rank + offset, 8)
        return (gx, y * 4 + lax.div(other_rank, 2), lax.rem(other_rank, 2))

    def y_peer(offset):
        return (gx, lax.rem(y + offset, 4) * 4 + in_row, sa)

    def z_peer(offset):
        return (lax.rem(gx + offset, 4), gz, sa)

    def gz_peer(offset):
        return (gx, lax.rem(gz + offset + 16, 16), sa)

    def loads():
        return [
            pltpu.make_async_copy(
                forcing.at[pl.ds(c0, nc)],
                field0.at[pl.ds(c0, nc), :, pl.ds(1, CELLS)],
                load_sem.at[g],
            )
            for g, (c0, nc, _) in enumerate(GROUPS)
        ]

    for copy in loads():
        copy.start()
    barrier = pltpu.get_barrier_semaphore()
    peers = [row_peer(d) for d in range(1, 8)]
    peers += [y_peer(d) for d in range(1, 4)] + [z_peer(d) for d in range(1, 4)]
    peers += [gz_peer(1), gz_peer(-1)]
    for peer in peers:
        pl.semaphore_signal(barrier, inc=1, device_id=peer, device_id_type=MESH)

    row = velocity[...]
    lane = lax.broadcasted_iota(jnp.int32, (1, NY), 1)
    after = pltpu.roll(row, NY - 1, 1)
    before = pltpu.roll(row, 1, 1)
    shear = jnp.where(
        lane == 0, after - row, jnp.where(lane == NY - 1, row - before, (after - before) * 0.5)
    )
    drift_row[...] = row * (0.5 * step_length)
    shear_row[...] = shear * step_length

    def split_into(target, value):
        high = value.astype(jnp.bfloat16)
        low = (value - high.astype(jnp.float32)).astype(jnp.bfloat16)
        target[pl.ds(0, NY), :] = high
        target[pl.ds(NY, NY), :] = high
        target[pl.ds(2 * NY, NY), :] = low

    split_into(solve, wall[...])
    split_into(solve_t, wall[...].T)
    squares[...] = jnp.zeros_like(squares)

    def split_rows(start, value):
        rows = value.shape[0] * value.shape[1]
        flat = value.reshape(rows, NY)
        high = flat.astype(jnp.bfloat16)
        low = (flat - high.astype(jnp.float32)).astype(jnp.bfloat16)
        lhs[pl.ds(start, rows), pl.ds(0, NY)] = high
        lhs[pl.ds(start, rows), pl.ds(NY, NY)] = low
        lhs[pl.ds(start, rows), pl.ds(2 * NY, NY)] = high

    def product(weights):
        return jnp.dot(lhs[...], weights[...], preferred_element_type=jnp.float32)

    def halo_copies(e, g, field):
        c0, nc, _ = GROUPS[g]
        part = pl.ds(c0, nc)

        def remote(k, src, dst, device):
            return pltpu.make_async_remote_copy(
                src_ref=src,
                dst_ref=dst,
                send_sem=send_sem.at[e, g, k],
                recv_sem=recv_sem.at[e, g, k],
                device_id=device,
                device_id_type=MESH,
            )

        return [
            remote(0, edge_out.at[e, 0, part], edge_in.at[e, 1, part], gz_peer(1)),
            remote(1, edge_out.at[e, 1, part], edge_in.at[e, 0, part], gz_peer(-1)),
            remote(2, field.at[part, :, CELLS], field.at[part, :, 0], z_peer(1)),
            remote(3, field.at[part, :, 1], field.at[part, :, CELLS + 1], z_peer(3)),
        ]

    def put_edges(e, c, b, cells, value):
        edge_out[e, 0, c, b, cells] = value[:, 7:8, :]
        edge_out[e, 1, c, b, cells] = value[:, 0:1, :]

    def stepped(e, g, field, extra, adjoint, x0):
        c0, nc, width = GROUPS[g]
        drift = drift_row[...].reshape(1, 1, NY)
        shear = shear_row[...].reshape(1, 1, NY)
        if adjoint:
            drift = -drift
        level = lax.broadcasted_iota(jnp.int32, (width, 8, NY), 1)
        out = {}
        for b in range(BLOCKS):
            centers = [field[c, b, pl.ds(x0 + 1, width)] for c in range(c0, c0 + nc)]
            for i in range(nc):
                c = c0 + i
                center = centers[i]
                east = field[c, b, pl.ds(x0 + 2, width)]
                west = field[c, b, pl.ds(x0, width)]
                north = jnp.where(
                    level == 7, edge_in[e, 0, c, b, pl.ds(x0, width)], pltpu.roll(center, 7, 1)
                )
                south = jnp.where(
                    level == 0, edge_in[e, 1, c, b, pl.ds(x0, width)], pltpu.roll(center, 1, 1)
                )
                value = (step_length * viscosity) * ((east + west) + (north + south))
                value = value + drift * (west - east)
                if extra is None:
                    value = value + (1.0 - 4.0 * step_length * viscosity + step_length) * center
                else:
                    value = value + (1.0 - 4.0 * step_length * viscosity) * center
                    value = value + step_length * extra(c, b, x0, width)
                if nc == 2 and i == (1 if adjoint else 0):
                    value = value - shear * centers[1 - i]
                out[i, b] = value
        return out

    def passes(g, body):
        width = GROUPS[g][2]

        def one(i, carry):
            body(pl.multiple_of(i * width, width))
            return carry

        lax.fori_loop(0, CELLS // width, one, 0)

    def run_group(g, body):
        c0, nc, width = GROUPS[g]
        tile = width * 8

        def step(x0):
            body(
                x0,
                lambda values: [
                    split_rows((i * BLOCKS + b) * tile, values[i, b])
                    for i in range(nc)
                    for b in range(BLOCKS)
                ],
                lambda weights: {
                    (i, b): value
                    for prod in [product(weights)]
                    for i in range(nc)
                    for b in range(BLOCKS)
                    for value in [
                        prod[(i * BLOCKS + b) * tile : (i * BLOCKS + b + 1) * tile].reshape(
                            width, 8, NY
                        )
                    ]
                },
            )

        passes(g, step)

    def put(e, g, field, values, x0):
        c0, nc, width = GROUPS[g]
        for i in range(nc):
            for b in range(BLOCKS):
                field[c0 + i, b, pl.ds(x0 + 1, width)] = values[i, b]
                put_edges(e, c0 + i, b, pl.ds(x0, width), values[i, b])

    for g, (c0, nc, width) in enumerate(GROUPS):
        loads()[g].wait()

        def edges(x0, c0=c0, nc=nc, width=width):
            for c in range(c0, c0 + nc):
                for b in range(BLOCKS):
                    put_edges(0, c, b, pl.ds(x0, width), field0[c, b, pl.ds(x0 + 1, width)])

        passes(g, edges)
        if g == 0:
            pl.semaphore_wait(barrier, len(peers))
        for copy in halo_copies(0, g, field0):
            copy.start()

    def arrived(e, g, field):
        for copy in halo_copies(e, g, field):
            copy.wait_recv()

    def send(e, g, field):
        for copy in halo_copies(e, g, field):
            copy.start()

    def forcing_at(c, b, x0, width):
        return field0[c, b, pl.ds(x0 + 1, width)]

    def held_at(c, b, x0, width):
        return held[c, b, pl.ds(x0, width)]

    for g in range(2):
        arrived(0, g, field0)

        def first(x0, spread, solved, g=g):
            spread(stepped(0, g, field0, None, False, x0))
            put(1, g, field1, solved(solve), x0)

        run_group(g, first)
        send(1, g, field1)

    for g in range(2):
        arrived(1, g, field1)

        def second(x0, spread, solved, g=g):
            c0, nc, width = GROUPS[g]
            spread(stepped(1, g, field1, forcing_at, False, x0))
            values = solved(solve)
            for b in range(BLOCKS):
                total = squares[b]
                for i in range(nc):
                    value = values[i, b]
                    held[c0 + i, b, pl.ds(x0, width)] = value
                    total = total + jnp.sum(value * value, axis=0)
                squares[b] = total
            spread(values)
            put(2, g, field2, solved(solve_t), x0)

        run_group(g, second)
        send(2, g, field2)

    for g in range(2):
        arrived(2, g, field2)

        def third(x0, spread, solved, g=g):
            spread(stepped(2, g, field2, held_at, True, x0))
            put(3, g, field3, solved(solve_t), x0)

        run_group(g, third)
        send(3, g, field3)

    def sketch_copy(c):
        return pltpu.make_async_remote_copy(
            src_ref=sketch.at[c],
            dst_ref=other.at[c],
            send_sem=sketch_send.at[c],
            recv_sem=sketch_recv.at[c],
            device_id=row_peer_sa,
            device_id_type=MESH,
        )

    row_peer_sa = (gx, gz, 1 - sa)
    for g, (c0, nc, width) in enumerate(GROUPS):
        arrived(3, g, field3)

        def fourth(x0, g=g, c0=c0, nc=nc, width=width):
            values = stepped(3, g, field3, held_at, True, x0)
            for i in range(nc):
                for b in range(BLOCKS):
                    sketch[c0 + i, b, pl.ds(x0, width)] = values[i, b]

        passes(g, fourth)

        @pl.when(sa == 0)
        def _(c0=c0, nc=nc):
            for c in range(c0, c0 + nc):
                sketch_copy(c).start()

    row_id = lax.broadcasted_iota(jnp.int32, (8, 128), 0)
    lane_id = lax.broadcasted_iota(jnp.int32, (8, 128), 1)

    def place(i, j, acc):
        total = jnp.sum(acc, axis=(0, 1), keepdims=True)
        return jnp.where((row_id == i) & (lane_id == j), total, 0.0)

    def products(c, accs, pairs, left, right):
        def one(x, accs):
            accs = list(accs)
            for half in range(2):
                part = pl.ds(half * 128, 128)
                a = [left[c, b, x, :, part] for b in range(BLOCKS)]
                d = a if right is left else [right[c, b, x, :, part] for b in range(BLOCKS)]
                for n, (i, j) in enumerate(pairs):
                    accs[n] = accs[n] + a[i] * d[j]
            return tuple(accs)

        return lax.fori_loop(0, CELLS, one, accs)

    own_pairs = [(i, j) for i in range(BLOCKS) for j in range(i, BLOCKS)]
    all_pairs = [(i, j) for i in range(BLOCKS) for j in range(BLOCKS)]
    zero = jnp.zeros((8, 128), jnp.float32)
    accs = tuple(zero for _ in own_pairs)
    for c in (2, 0, 1):
        accs = products(c, accs, own_pairs, sketch, sketch)
    tile = zero
    for n, (i, j) in enumerate(own_pairs):
        tile = tile + place(i + 4 * sa, j + 4 * sa, accs[n])
    for b in range(BLOCKS):
        square = squares[b]
        tile = tile + place(b + 4 * sa, 8, square[:, :128] + square[:, 128:])
    local_gram[...] = tile

    @pl.when(sa == 1)
    def _():
        accs = tuple(zero for _ in all_pairs)
        for c in (2, 0, 1):
            sketch_copy(c).wait_recv()
            accs = products(c, accs, all_pairs, other, sketch)
        tile = zero
        for n, (i, j) in enumerate(all_pairs):
            tile = tile + place(i, j + 4, accs[n])
        local_gram[...] += tile

    def sums(first_sem, buffer, me, peer, count):
        return [
            pltpu.make_async_remote_copy(
                src_ref=buffer.at[me],
                dst_ref=buffer.at[me],
                send_sem=sum_send.at[first_sem + d],
                recv_sem=sum_recv.at[first_sem + d],
                device_id=peer(d + 1),
                device_id_type=MESH,
            )
            for d in range(count - 1)
        ]

    total = local_gram[...]
    levels = [
        (0, row_sums, rank, row_peer, 8),
        (7, y_sums, y, y_peer, 4),
        (10, z_sums, gx, z_peer, 4),
    ]
    for first_sem, buffer, me, peer, count in levels:
        buffer[me] = total
        for copy in sums(first_sem, buffer, me, peer, count):
            copy.start()
        for copy in sums(first_sem, buffer, me, peer, count):
            copy.wait_recv()
        total = buffer[0]
        for k in range(1, count):
            total = total + buffer[k]

    for j in range(9):
        turned = total if j == 0 else pltpu.roll(total, 128 - j, 1)
        splats[j] = jnp.broadcast_to(turned[:, 0:1], (8, 128))
    scale = [jnp.sqrt(splats[8, i : i + 1] / entries + 1e-06) for i in range(8)]
    rows = []
    for p in range(8):
        current = {
            j: splats[j, p : p + 1] / entries / (scale[p] * scale[j]) for j in range(p, 8)
        }
        for q in range(p):
            current = {j: current[j] - rows[q][p] * rows[q][j] for j in current}
        root = jnp.sqrt(current[p])
        rows.append({j: current[j] / root for j in current})
    inverse = [None] * 8
    for p in range(7, -1, -1):
        current = {
            j: jnp.full((1, 128), 1.0 if j == p else 0.0, jnp.float32) for j in range(p, 8)
        }
        for q in range(p + 1, 8):
            for j in range(q, 8):
                current[j] = current[j] - rows[p][q] * inverse[q][j]
        inverse[p] = {j: current[j] / rows[p][p] for j in current}
    tile = zero
    for i in range(8):
        for j in range(i, 8):
            tile = tile + jnp.where((row_id == i) & (lane_id == j), rows[i][j], 0.0)
            coefs[i, pl.ds(j, 1)] = inverse[i][j] / scale[i]
    factor_out[...] = tile[:, :8]

    def stores():
        return [
            pltpu.make_async_copy(held.at[c], basis.at[c], store_sem.at[c]) for c in range(3)
        ]

    def write_basis(first, sources):
        weights = [
            [
                jnp.broadcast_to(coefs[i, pl.ds(first + j, 1)], (8, 128))
                if i <= first + j
                else None
                for j in range(BLOCKS)
            ]
            for i in range(len(sources) * BLOCKS)
        ]

        for c in range(3):

            def one(x, carry):
                for half in range(2):
                    part = pl.ds(half * 128, 128)
                    values = [s[c, b, x, :, part] for s in sources for b in range(BLOCKS)]
                    for j in range(BLOCKS):
                        acc = None
                        for i, value in enumerate(values):
                            if weights[i][j] is not None:
                                term = weights[i][j] * value
                                acc = term if acc is None else acc + term
                        held[c, j, x, :, part] = acc
                return carry

            lax.fori_loop(0, CELLS, one, 0)
            stores()[c].start()

    @pl.when(sa == 0)
    def _():
        write_basis(0, [sketch])

    @pl.when(sa == 1)
    def _():
        write_basis(4, [other, sketch])

    for copy in stores():
        copy.wait()
    for e, field in enumerate((field0, field1, field2, field3)):
        for g in range(2):
            for copy in halo_copies(e, g, field):
                copy.wait_send()

    @pl.when(sa == 0)
    def _():
        for c in range(3):
            sketch_copy(c).wait_send()

    for first_sem, buffer, me, peer, count in levels:
        for copy in sums(first_sem, buffer, me, peer, count):
            copy.wait_send()


def shards(forcing, velocity, wall_solve):
    f32, bf16 = jnp.float32, jnp.bfloat16
    entries = (
        3
        * forcing.shape[2]
        * lax.axis_size("gx")
        * forcing.shape[3]
        * lax.axis_size("gz")
        * forcing.shape[4]
    )
    tile = (3, BLOCKS, CELLS, 8, NY)
    padded = (3, BLOCKS, CELLS + 2, 8, NY)
    edges = (4, 2, 3, BLOCKS, CELLS, 1, NY)
    vmem = pl.BlockSpec(memory_space=pltpu.VMEM)
    hbm = pl.BlockSpec(memory_space=pl.ANY)
    return pl.pallas_call(
        functools.partial(kernel, float(entries)),
        out_shape=(jax.ShapeDtypeStruct(tile, f32), jax.ShapeDtypeStruct((8, 8), f32)),
        in_specs=[hbm, vmem, vmem],
        out_specs=(hbm, vmem),
        scratch_shapes=[
            pltpu.VMEM(padded, f32),
            pltpu.VMEM(padded, f32),
            pltpu.VMEM(padded, f32),
            pltpu.VMEM(padded, f32),
            pltpu.VMEM(tile, f32),
            pltpu.VMEM(tile, f32),
            pltpu.VMEM(tile, f32),
            pltpu.VMEM(edges, f32),
            pltpu.VMEM(edges, f32),
            pltpu.VMEM((ROWS, 3 * NY), bf16),
            pltpu.VMEM((3 * NY, NY), bf16),
            pltpu.VMEM((3 * NY, NY), bf16),
            pltpu.VMEM((1, NY), f32),
            pltpu.VMEM((1, NY), f32),
            pltpu.VMEM((BLOCKS, 8, NY), f32),
            pltpu.VMEM((8, 128), f32),
            pltpu.VMEM((8, 8, 128), f32),
            pltpu.VMEM((4, 8, 128), f32),
            pltpu.VMEM((4, 8, 128), f32),
            pltpu.VMEM((9, 8, 128), f32),
            pltpu.VMEM((8, 8, 128), f32),
            pltpu.SemaphoreType.DMA((2,)),
            pltpu.SemaphoreType.DMA((4, 2, 4)),
            pltpu.SemaphoreType.DMA((4, 2, 4)),
            pltpu.SemaphoreType.DMA((3,)),
            pltpu.SemaphoreType.DMA((3,)),
            pltpu.SemaphoreType.DMA((13,)),
            pltpu.SemaphoreType.DMA((13,)),
            pltpu.SemaphoreType.DMA((3,)),
        ],
        compiler_params=pltpu.CompilerParams(
            collective_id=0, has_side_effects=True, vmem_limit_bytes=56 << 20
        ),
        name="sketch",
    )(forcing, velocity.reshape(1, NY), wall_solve)


def solution(mesh):
    return jax.shard_map(
        shards,
        mesh=mesh,
        in_specs=(P(None, "sa", "gx", "gz", None), P(), P()),
        out_specs=(P(None, "sa", "gx", "gz", None), P()),
        check_vma=False,
    )
```

```python
import functools

import jax
import jax.numpy as jnp
from jax import lax
from jax.experimental import pallas as pl
from jax.experimental.pallas import tpu as pltpu
from jax.sharding import PartitionSpec as P

MESH = pl.DeviceIdType.MESH
step_length = 0.4
viscosity = 0.2
GROUPS = ((2, 1, 16), (0, 2, 8))
BLOCKS = 4
CELLS = 32
NY = 256
ROWS = 512


def kernel(
    entries,
    forcing,
    velocity,
    wall,
    basis,
    factor_out,
    field0,
    field1,
    field2,
    field3,
    held,
    sketch,
    other,
    edge_out,
    edge_in,
    lhs,
    solve,
    solve_t,
    drift_row,
    shear_row,
    squares,
    local_gram,
    row_sums,
    y_sums,
    z_sums,
    splats,
    coefs,
    load_sem,
    merge_send,
    merge_recv,
    send_sem,
    recv_sem,
    sketch_send,
    sketch_recv,
    relay_send,
    near_send,
    own_sem,
    sum_send,
    sum_recv,
    store_sem,
):
    gx, gz, sa = lax.axis_index("gx"), lax.axis_index("gz"), lax.axis_index("sa")
    in_row, y = lax.rem(gz, 4), lax.div(gz, 4)
    rank = in_row * 2 + sa

    def row_peer(offset):
        other_rank = lax.rem(rank + offset, 8)
        return (gx, y * 4 + lax.div(other_rank, 2), lax.rem(other_rank, 2))

    def y_peer(offset):
        return (gx, lax.rem(y + offset, 4) * 4 + in_row, sa)

    def z_peer(offset):
        return (lax.rem(gx + offset, 4), gz, sa)

    def gz_peer(offset):
        return (gx, lax.rem(gz + offset + 16, 16), sa)

    near = in_row + 1 - 2 * lax.rem(in_row, 2)
    far_first = 2 - 2 * lax.div(in_row, 2)
    near_first = 2 * lax.div(in_row, 2)

    def load(g, merged):
        part = pl.ds(*GROUPS[g][:2])
        if merged:
            return pltpu.make_async_copy(
                forcing.at[part, in_row],
                field0.at[part, in_row, pl.ds(1, CELLS)],
                load_sem.at[g],
            )
        return pltpu.make_async_copy(
            forcing.at[part], field0.at[part, :, pl.ds(1, CELLS)], load_sem.at[g]
        )

    def remote(src, dst, sent, received, device):
        return pltpu.make_async_remote_copy(
            src_ref=src,
            dst_ref=dst,
            send_sem=sent,
            recv_sem=received,
            device_id=device,
            device_id_type=MESH,
        )

    def merge_copy(g, d):
        part = pl.ds(*GROUPS[g][:2])
        column = lax.rem(in_row + d, 4)
        return remote(
            forcing.at[part, column],
            field0.at[part, in_row, pl.ds(1, CELLS)],
            merge_send.at[g, d - 1],
            merge_recv.at[g, d - 1],
            (gx, y * 4 + column, sa),
        )

    barrier = pltpu.get_barrier_semaphore()
    peers = [row_peer(d) for d in range(1, 8)]
    peers += [y_peer(d) for d in range(1, 4)] + [z_peer(d) for d in range(1, 4)]
    peers += [gz_peer(1), gz_peer(-1)]
    for peer in peers:
        pl.semaphore_signal(barrier, inc=1, device_id=peer, device_id_type=MESH)

    @pl.when(sa == 1)
    def _():
        for g in range(2):
            load(g, False).start()

    @pl.when(sa == 0)
    def _():
        for g in range(2):
            load(g, True).start()

    pl.semaphore_wait(barrier, len(peers))

    @pl.when(sa == 0)
    def _():
        for g in range(2):
            for d in (2, 3, 1):
                merge_copy(g, d).start()

    row = velocity[...]
    lane = lax.broadcasted_iota(jnp.int32, (1, NY), 1)
    after = pltpu.roll(row, NY - 1, 1)
    before = pltpu.roll(row, 1, 1)
    shear = jnp.where(
        lane == 0, after - row, jnp.where(lane == NY - 1, row - before, (after - before) * 0.5)
    )
    drift_row[...] = row * (0.5 * step_length)
    shear_row[...] = shear * step_length

    def split_into(target, value):
        high = value.astype(jnp.bfloat16)
        low = (value - high.astype(jnp.float32)).astype(jnp.bfloat16)
        target[pl.ds(0, NY), :] = high
        target[pl.ds(NY, NY), :] = high
        target[pl.ds(2 * NY, NY), :] = low

    split_into(solve, wall[...])
    split_into(solve_t, wall[...].T)
    squares[...] = jnp.zeros_like(squares)

    def split_rows(start, value):
        rows = value.shape[0] * value.shape[1]
        flat = value.reshape(rows, NY)
        high = flat.astype(jnp.bfloat16)
        low = (flat - high.astype(jnp.float32)).astype(jnp.bfloat16)
        lhs[pl.ds(start, rows), pl.ds(0, NY)] = high
        lhs[pl.ds(start, rows), pl.ds(NY, NY)] = low
        lhs[pl.ds(start, rows), pl.ds(2 * NY, NY)] = high

    def product(weights):
        return jnp.dot(lhs[...], weights[...], preferred_element_type=jnp.float32)

    def halo_copies(e, g, field, merged):
        part = pl.ds(*GROUPS[g][:2])

        def copy(k, src, dst, device):
            return remote(src, dst, send_sem.at[e, g, k], recv_sem.at[e, g, k], device)

        if merged:
            up, down = (edge_out.at[e, k, part, 0] for k in range(2))
            north, south = (edge_in.at[e, k, part, 0] for k in range(2))
            ahead, behind = y_peer(1), y_peer(3)
        else:
            up, down = (edge_out.at[e, k, part] for k in range(2))
            north, south = (edge_in.at[e, k, part] for k in range(2))
            ahead, behind = gz_peer(1), gz_peer(-1)
        return [
            copy(0, up, south, ahead),
            copy(1, down, north, behind),
            copy(2, field.at[part, :, CELLS], field.at[part, :, 0], z_peer(1)),
            copy(3, field.at[part, :, 1], field.at[part, :, CELLS + 1], z_peer(3)),
        ]

    def put_edges(e, c, b, cells, value, merged):
        if not merged:
            edge_out[e, 0, c, b, cells] = value[:, 7:8, :]
            edge_out[e, 1, c, b, cells] = value[:, 0:1, :]
        elif b == BLOCKS - 1:
            edge_out[e, 0, c, 0, cells] = value[:, 7:8, :]
        elif b == 0:
            edge_out[e, 1, c, 0, cells] = value[:, 0:1, :]

    def north_row(e, field, c, b, x0, width, merged):
        if merged and b < BLOCKS - 1:
            return field[c, b + 1, pl.ds(x0 + 1, width), 0:1, :]
        return edge_in[e, 0, c, 0 if merged else b, pl.ds(x0, width)]

    def south_row(e, field, c, b, x0, width, merged):
        if merged and b > 0:
            return field[c, b - 1, pl.ds(x0 + 1, width), 7:8, :]
        return edge_in[e, 1, c, 0 if merged else b, pl.ds(x0, width)]

    def stepped(e, g, field, extra, adjoint, x0, merged):
        c0, nc, width = GROUPS[g]
        drift = drift_row[...].reshape(1, 1, NY)
        shear = shear_row[...].reshape(1, 1, NY)
        if adjoint:
            drift = -drift
        level = lax.broadcasted_iota(jnp.int32, (width, 8, NY), 1)
        out = {}
        for b in range(BLOCKS):
            centers = [field[c, b, pl.ds(x0 + 1, width)] for c in range(c0, c0 + nc)]
            for i in range(nc):
                c = c0 + i
                center = centers[i]
                east = field[c, b, pl.ds(x0 + 2, width)]
                west = field[c, b, pl.ds(x0, width)]
                place = (e, field, c, b, x0, width, merged)
                north = jnp.where(level == 7, north_row(*place), pltpu.roll(center, 7, 1))
                south = jnp.where(level == 0, south_row(*place), pltpu.roll(center, 1, 1))
                value = (step_length * viscosity) * ((east + west) + (north + south))
                value = value + drift * (west - east)
                if extra is None:
                    value = value + (1.0 - 4.0 * step_length * viscosity + step_length) * center
                else:
                    value = value + (1.0 - 4.0 * step_length * viscosity) * center
                    value = value + step_length * extra(c, b, x0, width)
                if nc == 2 and i == (1 if adjoint else 0):
                    value = value - shear * centers[1 - i]
                out[i, b] = value
        return out

    def passes(g, body):
        width = GROUPS[g][2]

        def one(i, carry):
            body(pl.multiple_of(i * width, width))
            return carry

        lax.fori_loop(0, CELLS // width, one, 0)

    def run_group(g, body):
        c0, nc, width = GROUPS[g]
        tile = width * 8

        def step(x0):
            body(
                x0,
                lambda values: [
                    split_rows((i * BLOCKS + b) * tile, values[i, b])
                    for i in range(nc)
                    for b in range(BLOCKS)
                ],
                lambda weights: {
                    (i, b): value
                    for prod in [product(weights)]
                    for i in range(nc)
                    for b in range(BLOCKS)
                    for value in [
                        prod[(i * BLOCKS + b) * tile : (i * BLOCKS + b + 1) * tile].reshape(
                            width, 8, NY
                        )
                    ]
                },
            )

        passes(g, step)

    def put(e, g, field, values, x0, merged):
        c0, nc, width = GROUPS[g]
        for i in range(nc):
            for b in range(BLOCKS):
                field[c0 + i, b, pl.ds(x0 + 1, width)] = values[i, b]
                put_edges(e, c0 + i, b, pl.ds(x0, width), values[i, b], merged)

    def forcing_at(c, b, x0, width):
        return field0[c, b, pl.ds(x0 + 1, width)]

    def held_at(c, b, x0, width):
        return held[c, b, pl.ds(x0, width)]

    def chain(merged, finished):
        def arrived(e, g, field):
            for copy in halo_copies(e, g, field, merged):
                copy.wait_recv()

        def send(e, g, field):
            for copy in halo_copies(e, g, field, merged):
                copy.start()

        for g, (c0, nc, width) in enumerate(GROUPS):
            load(g, merged).wait()
            if merged:
                for d in (1, 2, 3):
                    merge_copy(g, d).wait_recv()

            def edges(x0, c0=c0, nc=nc, width=width):
                for c in range(c0, c0 + nc):
                    for b in (0, BLOCKS - 1) if merged else range(BLOCKS):
                        cells = pl.ds(x0, width)
                        put_edges(0, c, b, cells, field0[c, b, pl.ds(x0 + 1, width)], merged)

            passes(g, edges)
            send(0, g, field0)

        for g in range(2):
            arrived(0, g, field0)

            def first(x0, spread, solved, g=g):
                spread(stepped(0, g, field0, None, False, x0, merged))
                put(1, g, field1, solved(solve), x0, merged)

            run_group(g, first)
            send(1, g, field1)

        for g in range(2):
            arrived(1, g, field1)

            def second(x0, spread, solved, g=g):
                c0, nc, width = GROUPS[g]
                spread(stepped(1, g, field1, forcing_at, False, x0, merged))
                values = solved(solve)
                for b in range(BLOCKS):
                    total = squares[b]
                    for i in range(nc):
                        value = values[i, b]
                        held[c0 + i, b, pl.ds(x0, width)] = value
                        total = total + jnp.sum(value * value, axis=0)
                    squares[b] = total
                spread(values)
                put(2, g, field2, solved(solve_t), x0, merged)

            run_group(g, second)
            send(2, g, field2)

        for g in range(2):
            arrived(2, g, field2)

            def third(x0, spread, solved, g=g):
                spread(stepped(2, g, field2, held_at, True, x0, merged))
                put(3, g, field3, solved(solve_t), x0, merged)

            run_group(g, third)
            send(3, g, field3)

        for g, (c0, nc, width) in enumerate(GROUPS):
            arrived(3, g, field3)

            def fourth(x0, g=g, c0=c0, nc=nc, width=width):
                values = stepped(3, g, field3, held_at, True, x0, merged)
                for i in range(nc):
                    for b in range(BLOCKS):
                        sketch[c0 + i, b, pl.ds(x0, width)] = values[i, b]

            passes(g, fourth)
            for c in range(c0, c0 + nc):
                finished(c)

    def spread_copy(c, t):
        return remote(
            sketch.at[c, t],
            other.at[c, in_row],
            sketch_send.at[c, t],
            sketch_recv.at[c, in_row],
            (gx, y * 4 + t, 1),
        )

    def near_copy(c):
        return remote(
            sketch.at[c, near],
            other.at[c, in_row],
            near_send.at[c],
            sketch_recv.at[c, in_row],
            (gx, y * 4 + near, 0),
        )

    def relay_copy(c, k):
        return remote(
            other.at[c, k],
            other.at[c, k],
            relay_send.at[c, k],
            sketch_recv.at[c, k],
            (gx, gz, 0),
        )

    def own_copy(c):
        return pltpu.make_async_copy(sketch.at[c, in_row], other.at[c, in_row], own_sem.at[c])

    def sketch_wait(c, k):
        remote(
            other.at[c, k],
            other.at[c, k],
            relay_send.at[c, k],
            sketch_recv.at[c, k],
            (gx, gz, 1 - sa),
        ).wait_recv()

    def give(c):
        for k in range(2):
            spread_copy(c, far_first + k).start()
        for k in range(2):
            spread_copy(c, near_first + k).start()
        near_copy(c).start()
        own_copy(c).start()

    row_id = lax.broadcasted_iota(jnp.int32, (8, 128), 0)
    lane_id = lax.broadcasted_iota(jnp.int32, (8, 128), 1)
    zero = jnp.zeros((8, 128), jnp.float32)

    def place(i, j, acc):
        total = jnp.sum(acc, axis=(0, 1), keepdims=True)
        return jnp.where((row_id == i) & (lane_id == j), total, 0.0)

    def products(c, accs, pairs, sources):
        def one(x, accs):
            accs = list(accs)
            for half in range(2):
                part = pl.ds(half * 128, 128)
                values = [s[c, b, x, :, part] for s in sources for b in range(BLOCKS)]
                for n, (i, j) in enumerate(pairs):
                    accs[n] = accs[n] + values[i] * values[j]
            return tuple(accs)

        return lax.fori_loop(0, CELLS, one, accs)

    @pl.when(sa == 0)
    def _():
        chain(True, give)
        square = squares[0] + squares[1] + squares[2] + squares[3]
        local_gram[...] = place(in_row, 8, square[:, :128] + square[:, 128:])

    @pl.when(sa == 1)
    def _():
        chain(False, lambda c: None)
        own_pairs = [(i, j) for i in range(BLOCKS) for j in range(i, BLOCKS)]
        accs = tuple(zero for _ in own_pairs)
        for c in (2, 0, 1):
            accs = products(c, accs, own_pairs, [sketch])
        tile = zero
        for n, (i, j) in enumerate(own_pairs):
            tile = tile + place(i + 4, j + 4, accs[n])
        for b in range(BLOCKS):
            square = squares[b]
            tile = tile + place(b + 4, 8, square[:, :128] + square[:, 128:])
        local_gram[...] = tile
        pairs = [(i, j) for i in range(BLOCKS) for j in range(i, 2 * BLOCKS)]
        accs = tuple(zero for _ in pairs)
        for c in (2, 0, 1):
            for k in range(2):
                sketch_wait(c, far_first + k)
                relay_copy(c, far_first + k).start()
            for k in range(2):
                sketch_wait(c, near_first + k)
            accs = products(c, accs, pairs, [other, sketch])
        tile = zero
        for n, (i, j) in enumerate(pairs):
            tile = tile + place(i, j, accs[n])
        local_gram[...] += tile

    def sums(first_sem, buffer, me, peer, count):
        return [
            remote(
                buffer.at[me],
                buffer.at[me],
                sum_send.at[first_sem + d],
                sum_recv.at[first_sem + d],
                peer(d + 1),
            )
            for d in range(count - 1)
        ]

    total = local_gram[...]
    levels = [
        (0, row_sums, rank, row_peer, 8),
        (7, y_sums, y, y_peer, 4),
        (10, z_sums, gx, z_peer, 4),
    ]
    for first_sem, buffer, me, peer, count in levels:
        buffer[me] = total
        for copy in sums(first_sem, buffer, me, peer, count):
            copy.start()
        for copy in sums(first_sem, buffer, me, peer, count):
            copy.wait_recv()
        total = buffer[0]
        for k in range(1, count):
            total = total + buffer[k]

    for j in range(9):
        turned = total if j == 0 else pltpu.roll(total, 128 - j, 1)
        splats[j] = jnp.broadcast_to(turned[:, 0:1], (8, 128))
    scale = [jnp.sqrt(splats[8, i : i + 1] / entries + 1e-06) for i in range(8)]
    rows = []
    for p in range(8):
        current = {
            j: splats[j, p : p + 1] / entries / (scale[p] * scale[j]) for j in range(p, 8)
        }
        for q in range(p):
            current = {j: current[j] - rows[q][p] * rows[q][j] for j in current}
        root = jnp.sqrt(current[p])
        rows.append({j: current[j] / root for j in current})
    inverse = [None] * 8
    for p in range(7, -1, -1):
        current = {
            j: jnp.full((1, 128), 1.0 if j == p else 0.0, jnp.float32) for j in range(p, 8)
        }
        for q in range(p + 1, 8):
            for j in range(q, 8):
                current[j] = current[j] - rows[p][q] * inverse[q][j]
        inverse[p] = {j: current[j] / rows[p][p] for j in current}
    tile = zero
    for i in range(8):
        for j in range(i, 8):
            tile = tile + jnp.where((row_id == i) & (lane_id == j), rows[i][j], 0.0)
            coefs[i, pl.ds(j, 1)] = inverse[i][j] / scale[i]
    factor_out[...] = tile[:, :8]

    def store(c):
        return pltpu.make_async_copy(held.at[c], basis.at[c], store_sem.at[c])

    def write_basis(first, sources, ready):
        weights = [
            [
                jnp.broadcast_to(coefs[i, pl.ds(first + j, 1)], (8, 128))
                if i <= first + j
                else None
                for j in range(BLOCKS)
            ]
            for i in range(len(sources) * BLOCKS)
        ]

        for c in (2, 0, 1):
            ready(c)

            def one(x, carry):
                for half in range(2):
                    part = pl.ds(half * 128, 128)
                    values = [s[c, b, x, :, part] for s in sources for b in range(BLOCKS)]
                    for j in range(BLOCKS):
                        acc = None
                        for i, value in enumerate(values):
                            if weights[i][j] is not None:
                                term = weights[i][j] * value
                                acc = term if acc is None else acc + term
                        held[c, j, x, :, part] = acc
                return carry

            lax.fori_loop(0, CELLS, one, 0)
            store(c).start()

    def drain(merged):
        for e, field in enumerate((field0, field1, field2, field3)):
            for g in range(2):
                for copy in halo_copies(e, g, field, merged):
                    copy.wait_send()

    @pl.when(sa == 0)
    def _():
        def ready(c):
            own_copy(c).wait()
            for d in (1, 2, 3):
                sketch_wait(c, lax.rem(in_row + d, 4))

        write_basis(0, [other], ready)
        drain(True)
        for g in range(2):
            for d in (1, 2, 3):
                merge_copy(g, d).wait_send()
        for c in range(3):
            for t in range(BLOCKS):
                spread_copy(c, t).wait_send()
            near_copy(c).wait_send()

    @pl.when(sa == 1)
    def _():
        write_basis(4, [other, sketch], lambda c: None)
        drain(False)
        for c in range(3):
            for k in range(2):
                relay_copy(c, far_first + k).wait_send()

    for c in range(3):
        store(c).wait()
    for first_sem, buffer, me, peer, count in levels:
        for copy in sums(first_sem, buffer, me, peer, count):
            copy.wait_send()


def shards(forcing, velocity, wall_solve):
    f32, bf16 = jnp.float32, jnp.bfloat16
    entries = (
        3
        * forcing.shape[2]
        * lax.axis_size("gx")
        * forcing.shape[3]
        * lax.axis_size("gz")
        * forcing.shape[4]
    )
    tile = (3, BLOCKS, CELLS, 8, NY)
    padded = (3, BLOCKS, CELLS + 2, 8, NY)
    edges = (4, 2, 3, BLOCKS, CELLS, 1, NY)
    vmem = pl.BlockSpec(memory_space=pltpu.VMEM)
    hbm = pl.BlockSpec(memory_space=pl.ANY)
    return pl.pallas_call(
        functools.partial(kernel, float(entries)),
        out_shape=(jax.ShapeDtypeStruct(tile, f32), jax.ShapeDtypeStruct((8, 8), f32)),
        in_specs=[hbm, vmem, vmem],
        out_specs=(hbm, vmem),
        scratch_shapes=[
            pltpu.VMEM(padded, f32),
            pltpu.VMEM(padded, f32),
            pltpu.VMEM(padded, f32),
            pltpu.VMEM(padded, f32),
            pltpu.VMEM(tile, f32),
            pltpu.VMEM(tile, f32),
            pltpu.VMEM(tile, f32),
            pltpu.VMEM(edges, f32),
            pltpu.VMEM(edges, f32),
            pltpu.VMEM((ROWS, 3 * NY), bf16),
            pltpu.VMEM((3 * NY, NY), bf16),
            pltpu.VMEM((3 * NY, NY), bf16),
            pltpu.VMEM((1, NY), f32),
            pltpu.VMEM((1, NY), f32),
            pltpu.VMEM((BLOCKS, 8, NY), f32),
            pltpu.VMEM((8, 128), f32),
            pltpu.VMEM((8, 8, 128), f32),
            pltpu.VMEM((4, 8, 128), f32),
            pltpu.VMEM((4, 8, 128), f32),
            pltpu.VMEM((9, 8, 128), f32),
            pltpu.VMEM((8, 8, 128), f32),
            pltpu.SemaphoreType.DMA((2,)),
            pltpu.SemaphoreType.DMA((2, 3)),
            pltpu.SemaphoreType.DMA((2, 3)),
            pltpu.SemaphoreType.DMA((4, 2, 4)),
            pltpu.SemaphoreType.DMA((4, 2, 4)),
            pltpu.SemaphoreType.DMA((3, 4)),
            pltpu.SemaphoreType.DMA((3, 4)),
            pltpu.SemaphoreType.DMA((3, 4)),
            pltpu.SemaphoreType.DMA((3,)),
            pltpu.SemaphoreType.DMA((3,)),
            pltpu.SemaphoreType.DMA((13,)),
            pltpu.SemaphoreType.DMA((13,)),
            pltpu.SemaphoreType.DMA((3,)),
        ],
        compiler_params=pltpu.CompilerParams(
            collective_id=0, has_side_effects=True, vmem_limit_bytes=56 << 20
        ),
        name="sketch",
    )(forcing, velocity.reshape(1, NY), wall_solve)


def solution(mesh):
    return jax.shard_map(
        shards,
        mesh=mesh,
        in_specs=(P(None, "sa", "gx", "gz", None), P(), P()),
        out_specs=(P(None, "sa", "gx", "gz", None), P()),
        check_vma=False,
    )
```

```python
import functools

import jax
import jax.numpy as jnp
from jax import lax
from jax.experimental import pallas as pl
from jax.experimental.pallas import tpu as pltpu
from jax.sharding import PartitionSpec as P

MESH = pl.DeviceIdType.MESH
step_length = 0.4
viscosity = 0.2
GROUPS = ((2, 1, 16), (0, 2, 8))
BLOCKS = 4
CELLS = 32
NY = 256
ROWS = 512


def kernel(
    entries,
    forcing,
    velocity,
    wall,
    basis,
    factor_out,
    field0,
    field1,
    field2,
    field3,
    held,
    sketch,
    other,
    edge_out,
    edge_in,
    lhs,
    solve,
    solve_t,
    drift_row,
    shear_row,
    squares,
    local_gram,
    row_sums,
    y_sums,
    z_sums,
    splats,
    coefs,
    load_sem,
    merge_send,
    merge_recv,
    send_sem,
    recv_sem,
    sketch_send,
    sketch_recv,
    relay_send,
    near_send,
    own_sem,
    sum_send,
    sum_recv,
    store_sem,
):
    gx, gz, sa = lax.axis_index("gx"), lax.axis_index("gz"), lax.axis_index("sa")
    in_row, y = lax.rem(gz, 4), lax.div(gz, 4)
    rank = in_row * 2 + sa

    def row_peer(offset):
        other_rank = lax.rem(rank + offset, 8)
        return (gx, y * 4 + lax.div(other_rank, 2), lax.rem(other_rank, 2))

    def y_peer(offset):
        return (gx, lax.rem(y + offset, 4) * 4 + in_row, sa)

    def z_peer(offset):
        return (lax.rem(gx + offset, 4), gz, sa)

    def gz_peer(offset):
        return (gx, lax.rem(gz + offset + 16, 16), sa)

    near = in_row + 1 - 2 * lax.rem(in_row, 2)
    far_first = 2 - 2 * lax.div(in_row, 2)
    near_first = 2 * lax.div(in_row, 2)

    def load(g, merged):
        part = pl.ds(*GROUPS[g][:2])
        if merged:
            return pltpu.make_async_copy(
                forcing.at[part, in_row],
                field0.at[part, in_row, pl.ds(1, CELLS)],
                load_sem.at[g],
            )
        return pltpu.make_async_copy(
            forcing.at[part], field0.at[part, :, pl.ds(1, CELLS)], load_sem.at[g]
        )

    def remote(src, dst, sent, received, device):
        return pltpu.make_async_remote_copy(
            src_ref=src,
            dst_ref=dst,
            send_sem=sent,
            recv_sem=received,
            device_id=device,
            device_id_type=MESH,
        )

    def merge_copy(g, d):
        part = pl.ds(*GROUPS[g][:2])
        column = lax.rem(in_row + d, 4)
        return remote(
            forcing.at[part, column],
            field0.at[part, in_row, pl.ds(1, CELLS)],
            merge_send.at[g, d - 1],
            merge_recv.at[g, d - 1],
            (gx, y * 4 + column, sa),
        )

    barrier = pltpu.get_barrier_semaphore()
    peers = [row_peer(d) for d in range(1, 8)]
    peers += [y_peer(d) for d in range(1, 4)] + [z_peer(d) for d in range(1, 4)]
    peers += [gz_peer(1), gz_peer(-1)]
    for peer in peers:
        pl.semaphore_signal(barrier, inc=1, device_id=peer, device_id_type=MESH)

    @pl.when(sa == 1)
    def _():
        for g in range(2):
            load(g, False).start()

    @pl.when(sa == 0)
    def _():
        for g in range(2):
            load(g, True).start()

    pl.semaphore_wait(barrier, len(peers))

    @pl.when(sa == 0)
    def _():
        for g in range(2):
            for d in (2, 3, 1):
                merge_copy(g, d).start()

    row = velocity[...]
    lane = lax.broadcasted_iota(jnp.int32, (1, NY), 1)
    after = pltpu.roll(row, NY - 1, 1)
    before = pltpu.roll(row, 1, 1)
    shear = jnp.where(
        lane == 0, after - row, jnp.where(lane == NY - 1, row - before, (after - before) * 0.5)
    )
    drift_row[...] = row * (0.5 * step_length)
    shear_row[...] = shear * step_length

    def split_into(target, value):
        high = value.astype(jnp.bfloat16)
        low = (value - high.astype(jnp.float32)).astype(jnp.bfloat16)
        target[pl.ds(0, NY), :] = high
        target[pl.ds(NY, NY), :] = high
        target[pl.ds(2 * NY, NY), :] = low

    split_into(solve, wall[...])
    split_into(solve_t, wall[...].T)
    squares[...] = jnp.zeros_like(squares)

    def split_rows(start, value):
        rows = value.shape[0] * value.shape[1]
        flat = value.reshape(rows, NY)
        high = flat.astype(jnp.bfloat16)
        low = (flat - high.astype(jnp.float32)).astype(jnp.bfloat16)
        lhs[pl.ds(start, rows), pl.ds(0, NY)] = high
        lhs[pl.ds(start, rows), pl.ds(NY, NY)] = low
        lhs[pl.ds(start, rows), pl.ds(2 * NY, NY)] = high

    def product(weights):
        return jnp.dot(lhs[...], weights[...], preferred_element_type=jnp.float32)

    def halo_copy(e, g, field, merged, k):
        part = pl.ds(*GROUPS[g][:2])
        if k < 4:
            half, way = divmod(k, 2)
            cells = pl.ds(half * (CELLS // 2), CELLS // 2)
            if merged:
                src = edge_out.at[e, way, part, 0, cells]
                dst = edge_in.at[e, 1 - way, part, 0, cells]
                device = y_peer(3) if way else y_peer(1)
            else:
                src = edge_out.at[e, way, part, :, cells]
                dst = edge_in.at[e, 1 - way, part, :, cells]
                device = gz_peer(-1) if way else gz_peer(1)
        elif k == 4:
            src, dst, device = field.at[part, :, CELLS], field.at[part, :, 0], z_peer(1)
        else:
            src, dst, device = field.at[part, :, 1], field.at[part, :, CELLS + 1], z_peer(3)
        return remote(src, dst, send_sem.at[e, g, k], recv_sem.at[e, g, k], device)

    def put_edges(e, c, b, cells, value, merged):
        if not merged:
            edge_out[e, 0, c, b, cells] = value[:, 7:8, :]
            edge_out[e, 1, c, b, cells] = value[:, 0:1, :]
        elif b == BLOCKS - 1:
            edge_out[e, 0, c, 0, cells] = value[:, 7:8, :]
        elif b == 0:
            edge_out[e, 1, c, 0, cells] = value[:, 0:1, :]

    def north_row(e, field, c, b, x0, p0, width, merged):
        if merged and b < BLOCKS - 1:
            return field[c, b + 1, pl.ds(x0 + 1, width), 0:1, :]
        return edge_in[e, 0, c, 0 if merged else b, pl.ds(p0, width)]

    def south_row(e, field, c, b, x0, p0, width, merged):
        if merged and b > 0:
            return field[c, b - 1, pl.ds(x0 + 1, width), 7:8, :]
        return edge_in[e, 1, c, 0 if merged else b, pl.ds(p0, width)]

    def stepped(e, g, field, extra, adjoint, x0, p0, merged):
        c0, nc, width = GROUPS[g]
        drift = drift_row[...].reshape(1, 1, NY)
        shear = shear_row[...].reshape(1, 1, NY)
        if adjoint:
            drift = -drift
        level = lax.broadcasted_iota(jnp.int32, (width, 8, NY), 1)
        out = {}
        for b in range(BLOCKS):
            centers = [field[c, b, pl.ds(x0 + 1, width)] for c in range(c0, c0 + nc)]
            for i in range(nc):
                c = c0 + i
                center = centers[i]
                east = field[c, b, pl.ds(x0 + 2, width)]
                west = field[c, b, pl.ds(x0, width)]
                place = (e, field, c, b, x0, p0, width, merged)
                north = jnp.where(level == 7, north_row(*place), pltpu.roll(center, 7, 1))
                south = jnp.where(level == 0, south_row(*place), pltpu.roll(center, 1, 1))
                value = (step_length * viscosity) * ((east + west) + (north + south))
                value = value + drift * (west - east)
                if extra is None:
                    value = value + (1.0 - 4.0 * step_length * viscosity + step_length) * center
                else:
                    value = value + (1.0 - 4.0 * step_length * viscosity) * center
                    value = value + step_length * extra(c, b, x0, width)
                if nc == 2 and i == (1 if adjoint else 0):
                    value = value - shear * centers[1 - i]
                out[i, b] = value
        return out

    def passes(g, body, merged, source=None, target=None):
        width = GROUPS[g][2]
        count = CELLS // width
        if count == 2:
            needed = {0: (0, 1, 4), 1: (2, 3, 5)}
            made = {0: (0, 1, 5), 1: (2, 3, 4)}
        else:
            needed = {0: (0, 1, 4, 5), 2: (2, 3)}
            made = {1: (0, 1, 4, 5), 3: (2, 3)}

        def one(i, carry):
            if count == 2:
                x0 = i * width
            else:
                x0 = lax.select(i < 2, i * (CELLS - width), (i - 1) * width)
            if source is not None:
                for at, copies in needed.items():

                    @pl.when(i == at)
                    def _(copies=copies):
                        for k in copies:
                            halo_copy(*source, merged, k).wait_recv()

            body(pl.multiple_of(x0, width), pl.multiple_of(i * width, width))
            if target is not None:
                for at, copies in made.items():

                    @pl.when(i == at)
                    def _(copies=copies):
                        for k in copies:
                            halo_copy(*target, merged, k).start()

            return carry

        lax.fori_loop(0, count, one, 0)

    def run_group(g, body, merged, source, target):
        c0, nc, width = GROUPS[g]
        tile = width * 8

        def spread(values):
            for i in range(nc):
                for b in range(BLOCKS):
                    split_rows((i * BLOCKS + b) * tile, values[i, b])

        def solved(weights):
            prod = product(weights)
            return {
                (i, b): prod[(i * BLOCKS + b) * tile : (i * BLOCKS + b + 1) * tile].reshape(
                    width, 8, NY
                )
                for i in range(nc)
                for b in range(BLOCKS)
            }

        passes(g, lambda x0, p0: body(x0, p0, spread, solved), merged, source, target)

    def put(e, g, field, values, x0, p0, merged):
        c0, nc, width = GROUPS[g]
        for i in range(nc):
            for b in range(BLOCKS):
                field[c0 + i, b, pl.ds(x0 + 1, width)] = values[i, b]
                put_edges(e, c0 + i, b, pl.ds(p0, width), values[i, b], merged)

    def forcing_at(c, b, x0, width):
        return field0[c, b, pl.ds(x0 + 1, width)]

    def held_at(c, b, x0, width):
        return held[c, b, pl.ds(x0, width)]

    def chain(merged, finished):
        def start(g):
            c0, nc, width = GROUPS[g]
            load(g, merged).wait()
            if merged:
                for d in (1, 2, 3):
                    merge_copy(g, d).wait_recv()

            def edges(x0, p0):
                for c in range(c0, c0 + nc):
                    for b in (0, BLOCKS - 1) if merged else range(BLOCKS):
                        value = field0[c, b, pl.ds(x0 + 1, width)]
                        put_edges(0, c, b, pl.ds(p0, width), value, merged)

            passes(g, edges, merged, target=(0, g, field0))

        def first(g):
            def body(x0, p0, spread, solved):
                spread(stepped(0, g, field0, None, False, x0, p0, merged))
                put(1, g, field1, solved(solve), x0, p0, merged)

            run_group(g, body, merged, (0, g, field0), (1, g, field1))

        def second(g):
            c0, nc, width = GROUPS[g]

            def body(x0, p0, spread, solved):
                spread(stepped(1, g, field1, forcing_at, False, x0, p0, merged))
                values = solved(solve)
                for b in range(BLOCKS):
                    total = squares[b]
                    for i in range(nc):
                        value = values[i, b]
                        held[c0 + i, b, pl.ds(x0, width)] = value
                        total = total + jnp.sum(value * value, axis=0)
                    squares[b] = total
                spread(values)
                put(2, g, field2, solved(solve_t), x0, p0, merged)

            run_group(g, body, merged, (1, g, field1), (2, g, field2))

        def third(g):
            def body(x0, p0, spread, solved):
                spread(stepped(2, g, field2, held_at, True, x0, p0, merged))
                put(3, g, field3, solved(solve_t), x0, p0, merged)

            run_group(g, body, merged, (2, g, field2), (3, g, field3))

        def fourth(g):
            c0, nc, width = GROUPS[g]

            def body(x0, p0):
                values = stepped(3, g, field3, held_at, True, x0, p0, merged)
                for i in range(nc):
                    for b in range(BLOCKS):
                        sketch[c0 + i, b, pl.ds(x0, width)] = values[i, b]

            passes(g, body, merged, source=(3, g, field3))
            for c in range(c0, c0 + nc):
                finished(c)

        stages = (start, first, second, third, fourth)
        if merged:
            order = [(stage, g) for g in range(2) for stage in stages]
        else:
            order = [(stage, g) for stage in stages for g in range(2)]
        for stage, g in order:
            stage(g)

    def spread_copy(c, t):
        return remote(
            sketch.at[c, t],
            other.at[c, in_row],
            sketch_send.at[c, t],
            sketch_recv.at[c, in_row],
            (gx, y * 4 + t, 1),
        )

    def near_copy(c):
        return remote(
            sketch.at[c, near],
            other.at[c, in_row],
            near_send.at[c],
            sketch_recv.at[c, in_row],
            (gx, y * 4 + near, 0),
        )

    def relay_copy(c, k):
        return remote(
            other.at[c, k],
            other.at[c, k],
            relay_send.at[c, k],
            sketch_recv.at[c, k],
            (gx, gz, 0),
        )

    def own_copy(c):
        return pltpu.make_async_copy(sketch.at[c, in_row], other.at[c, in_row], own_sem.at[c])

    def sketch_wait(c, k):
        remote(
            other.at[c, k],
            other.at[c, k],
            relay_send.at[c, k],
            sketch_recv.at[c, k],
            (gx, gz, 1 - sa),
        ).wait_recv()

    def give(c):
        for k in range(2):
            spread_copy(c, far_first + k).start()
        for k in range(2):
            spread_copy(c, near_first + k).start()
        near_copy(c).start()
        own_copy(c).start()

    row_id = lax.broadcasted_iota(jnp.int32, (8, 128), 0)
    lane_id = lax.broadcasted_iota(jnp.int32, (8, 128), 1)
    zero = jnp.zeros((8, 128), jnp.float32)

    def place(i, j, acc):
        total = jnp.sum(acc, axis=(0, 1), keepdims=True)
        return jnp.where((row_id == i) & (lane_id == j), total, 0.0)

    def products(c, accs, pairs, sources):
        def one(x, accs):
            accs = list(accs)
            for half in range(2):
                part = pl.ds(half * 128, 128)
                values = [s[c, b, x, :, part] for s in sources for b in range(BLOCKS)]
                for n, (i, j) in enumerate(pairs):
                    accs[n] = accs[n] + values[i] * values[j]
            return tuple(accs)

        return lax.fori_loop(0, CELLS, one, accs)

    @pl.when(sa == 0)
    def _():
        chain(True, give)
        square = squares[0] + squares[1] + squares[2] + squares[3]
        local_gram[...] = place(in_row, 8, square[:, :128] + square[:, 128:])

    @pl.when(sa == 1)
    def _():
        chain(False, lambda c: None)
        own_pairs = [(i, j) for i in range(BLOCKS) for j in range(i, BLOCKS)]
        accs = tuple(zero for _ in own_pairs)
        for c in (2, 0, 1):
            accs = products(c, accs, own_pairs, [sketch])
        tile = zero
        for n, (i, j) in enumerate(own_pairs):
            tile = tile + place(i + 4, j + 4, accs[n])
        for b in range(BLOCKS):
            square = squares[b]
            tile = tile + place(b + 4, 8, square[:, :128] + square[:, 128:])
        local_gram[...] = tile
        pairs = [(i, j) for i in range(BLOCKS) for j in range(i, 2 * BLOCKS)]
        accs = tuple(zero for _ in pairs)
        for c in (2, 0, 1):
            for k in range(2):
                sketch_wait(c, far_first + k)
                relay_copy(c, far_first + k).start()
            for k in range(2):
                sketch_wait(c, near_first + k)
            accs = products(c, accs, pairs, [other, sketch])
        tile = zero
        for n, (i, j) in enumerate(pairs):
            tile = tile + place(i, j, accs[n])
        local_gram[...] += tile

    def sums(first_sem, buffer, me, peer, count):
        return [
            remote(
                buffer.at[me],
                buffer.at[me],
                sum_send.at[first_sem + d],
                sum_recv.at[first_sem + d],
                peer(d + 1),
            )
            for d in range(count - 1)
        ]

    total = local_gram[...]
    levels = [
        (0, row_sums, rank, row_peer, 8),
        (7, y_sums, y, y_peer, 4),
        (10, z_sums, gx, z_peer, 4),
    ]
    for first_sem, buffer, me, peer, count in levels:
        buffer[me] = total
        for copy in sums(first_sem, buffer, me, peer, count):
            copy.start()
        for copy in sums(first_sem, buffer, me, peer, count):
            copy.wait_recv()
        total = buffer[0]
        for k in range(1, count):
            total = total + buffer[k]

    for j in range(9):
        turned = total if j == 0 else pltpu.roll(total, 128 - j, 1)
        splats[j] = jnp.broadcast_to(turned[:, 0:1], (8, 128))
    scale = [jnp.sqrt(splats[8, i : i + 1] / entries + 1e-06) for i in range(8)]
    rows = []
    for p in range(8):
        current = {
            j: splats[j, p : p + 1] / entries / (scale[p] * scale[j]) for j in range(p, 8)
        }
        for q in range(p):
            current = {j: current[j] - rows[q][p] * rows[q][j] for j in current}
        root = jnp.sqrt(current[p])
        rows.append({j: current[j] / root for j in current})
    inverse = [None] * 8
    for p in range(7, -1, -1):
        current = {
            j: jnp.full((1, 128), 1.0 if j == p else 0.0, jnp.float32) for j in range(p, 8)
        }
        for q in range(p + 1, 8):
            for j in range(q, 8):
                current[j] = current[j] - rows[p][q] * inverse[q][j]
        inverse[p] = {j: current[j] / rows[p][p] for j in current}
    tile = zero
    for i in range(8):
        for j in range(i, 8):
            tile = tile + jnp.where((row_id == i) & (lane_id == j), rows[i][j], 0.0)
            coefs[i, pl.ds(j, 1)] = inverse[i][j] / scale[i]
    factor_out[...] = tile[:, :8]

    def store(c):
        return pltpu.make_async_copy(held.at[c], basis.at[c], store_sem.at[c])

    def write_basis(first, sources, ready):
        weights = [
            [
                jnp.broadcast_to(coefs[i, pl.ds(first + j, 1)], (8, 128))
                if i <= first + j
                else None
                for j in range(BLOCKS)
            ]
            for i in range(len(sources) * BLOCKS)
        ]

        for c in (2, 0, 1):
            ready(c)

            def one(x, carry):
                for half in range(2):
                    part = pl.ds(half * 128, 128)
                    values = [s[c, b, x, :, part] for s in sources for b in range(BLOCKS)]
                    for j in range(BLOCKS):
                        acc = None
                        for i, value in enumerate(values):
                            if weights[i][j] is not None:
                                term = weights[i][j] * value
                                acc = term if acc is None else acc + term
                        held[c, j, x, :, part] = acc
                return carry

            lax.fori_loop(0, CELLS, one, 0)
            store(c).start()

    def drain(merged):
        for e, field in enumerate((field0, field1, field2, field3)):
            for g in range(2):
                for k in range(6):
                    halo_copy(e, g, field, merged, k).wait_send()

    @pl.when(sa == 0)
    def _():
        def ready(c):
            own_copy(c).wait()
            for d in (1, 2, 3):
                sketch_wait(c, lax.rem(in_row + d, 4))

        write_basis(0, [other], ready)
        drain(True)
        for g in range(2):
            for d in (1, 2, 3):
                merge_copy(g, d).wait_send()
        for c in range(3):
            for t in range(BLOCKS):
                spread_copy(c, t).wait_send()
            near_copy(c).wait_send()

    @pl.when(sa == 1)
    def _():
        write_basis(4, [other, sketch], lambda c: None)
        drain(False)
        for c in range(3):
            for k in range(2):
                relay_copy(c, far_first + k).wait_send()

    for c in range(3):
        store(c).wait()
    for first_sem, buffer, me, peer, count in levels:
        for copy in sums(first_sem, buffer, me, peer, count):
            copy.wait_send()


def shards(forcing, velocity, wall_solve):
    f32, bf16 = jnp.float32, jnp.bfloat16
    entries = (
        3
        * forcing.shape[2]
        * lax.axis_size("gx")
        * forcing.shape[3]
        * lax.axis_size("gz")
        * forcing.shape[4]
    )
    tile = (3, BLOCKS, CELLS, 8, NY)
    padded = (3, BLOCKS, CELLS + 2, 8, NY)
    edges = (4, 2, 3, BLOCKS, CELLS, 1, NY)
    vmem = pl.BlockSpec(memory_space=pltpu.VMEM)
    hbm = pl.BlockSpec(memory_space=pl.ANY)
    return pl.pallas_call(
        functools.partial(kernel, float(entries)),
        out_shape=(jax.ShapeDtypeStruct(tile, f32), jax.ShapeDtypeStruct((8, 8), f32)),
        in_specs=[hbm, vmem, vmem],
        out_specs=(hbm, vmem),
        scratch_shapes=[
            pltpu.VMEM(padded, f32),
            pltpu.VMEM(padded, f32),
            pltpu.VMEM(padded, f32),
            pltpu.VMEM(padded, f32),
            pltpu.VMEM(tile, f32),
            pltpu.VMEM(tile, f32),
            pltpu.VMEM(tile, f32),
            pltpu.VMEM(edges, f32),
            pltpu.VMEM(edges, f32),
            pltpu.VMEM((ROWS, 3 * NY), bf16),
            pltpu.VMEM((3 * NY, NY), bf16),
            pltpu.VMEM((3 * NY, NY), bf16),
            pltpu.VMEM((1, NY), f32),
            pltpu.VMEM((1, NY), f32),
            pltpu.VMEM((BLOCKS, 8, NY), f32),
            pltpu.VMEM((8, 128), f32),
            pltpu.VMEM((8, 8, 128), f32),
            pltpu.VMEM((4, 8, 128), f32),
            pltpu.VMEM((4, 8, 128), f32),
            pltpu.VMEM((9, 8, 128), f32),
            pltpu.VMEM((8, 8, 128), f32),
            pltpu.SemaphoreType.DMA((2,)),
            pltpu.SemaphoreType.DMA((2, 3)),
            pltpu.SemaphoreType.DMA((2, 3)),
            pltpu.SemaphoreType.DMA((4, 2, 6)),
            pltpu.SemaphoreType.DMA((4, 2, 6)),
            pltpu.SemaphoreType.DMA((3, 4)),
            pltpu.SemaphoreType.DMA((3, 4)),
            pltpu.SemaphoreType.DMA((3, 4)),
            pltpu.SemaphoreType.DMA((3,)),
            pltpu.SemaphoreType.DMA((3,)),
            pltpu.SemaphoreType.DMA((13,)),
            pltpu.SemaphoreType.DMA((13,)),
            pltpu.SemaphoreType.DMA((3,)),
        ],
        compiler_params=pltpu.CompilerParams(
            collective_id=0, has_side_effects=True, vmem_limit_bytes=56 << 20
        ),
        name="sketch",
    )(forcing, velocity.reshape(1, NY), wall_solve)


def solution(mesh):
    return jax.shard_map(
        shards,
        mesh=mesh,
        in_specs=(P(None, "sa", "gx", "gz", None), P(), P()),
        out_specs=(P(None, "sa", "gx", "gz", None), P()),
        check_vma=False,
    )
```

```python
import functools

import jax
import jax.numpy as jnp
from jax import lax
from jax.experimental import pallas as pl
from jax.experimental.pallas import tpu as pltpu
from jax.sharding import PartitionSpec as P

MESH = pl.DeviceIdType.MESH
step_length = 0.4
viscosity = 0.2
GROUPS = ((2, 1, 16), (0, 2, 8))
BLOCKS = 4
CELLS = 32
NY = 256
HALF = 256


def kernel(
    forcing,
    velocity,
    wall,
    other_out,
    sketch_out,
    gram_out,
    field0,
    field1,
    field2,
    field3,
    held,
    sketch,
    other,
    edge_out,
    edge_in,
    lhs0,
    lhs1,
    solve,
    solve_t,
    drift_row,
    shear_row,
    squares,
    local_gram,
    row_sums,
    plane_sums,
    load_sem,
    merge_send,
    merge_recv,
    send_sem,
    recv_sem,
    sketch_send,
    sketch_recv,
    relay_send,
    near_send,
    own_sem,
    sum_send,
    sum_recv,
    store_sem,
):
    gx, gz, sa = lax.axis_index("gx"), lax.axis_index("gz"), lax.axis_index("sa")
    in_row, y = lax.rem(gz, 4), lax.div(gz, 4)
    rank = in_row * 2 + sa

    def row_peer(offset):
        other_rank = lax.rem(rank + offset, 8)
        return (gx, y * 4 + lax.div(other_rank, 2), lax.rem(other_rank, 2))

    def y_peer(offset):
        return (gx, lax.rem(y + offset, 4) * 4 + in_row, sa)

    def z_peer(offset):
        return (lax.rem(gx + offset, 4), gz, sa)

    def plane_peer(offset):
        place = lax.rem(gx * 4 + y + offset, 16)
        return (lax.div(place, 4), lax.rem(place, 4) * 4 + in_row, sa)

    def gz_peer(offset):
        return (gx, lax.rem(gz + offset + 16, 16), sa)

    near = in_row + 1 - 2 * lax.rem(in_row, 2)
    far_first = 2 - 2 * lax.div(in_row, 2)
    near_first = 2 * lax.div(in_row, 2)

    def load(g, merged):
        part = pl.ds(*GROUPS[g][:2])
        if merged:
            return pltpu.make_async_copy(
                forcing.at[part, in_row],
                field0.at[part, in_row, pl.ds(1, CELLS)],
                load_sem.at[g],
            )
        return pltpu.make_async_copy(
            forcing.at[part], field0.at[part, :, pl.ds(1, CELLS)], load_sem.at[g]
        )

    def remote(src, dst, sent, received, device):
        return pltpu.make_async_remote_copy(
            src_ref=src,
            dst_ref=dst,
            send_sem=sent,
            recv_sem=received,
            device_id=device,
            device_id_type=MESH,
        )

    def merge_copy(g, d):
        part = pl.ds(*GROUPS[g][:2])
        column = lax.rem(in_row + d, 4)
        return remote(
            forcing.at[part, column],
            field0.at[part, in_row, pl.ds(1, CELLS)],
            merge_send.at[g, d - 1],
            merge_recv.at[g, d - 1],
            (gx, y * 4 + column, sa),
        )

    barrier = pltpu.get_barrier_semaphore()
    peers = [row_peer(d) for d in range(1, 8)]
    peers += [plane_peer(d) for d in range(1, 16)]
    peers += [gz_peer(1), gz_peer(-1)]
    for peer in peers:
        pl.semaphore_signal(barrier, inc=1, device_id=peer, device_id_type=MESH)

    @pl.when(sa == 1)
    def _():
        for g in range(2):
            load(g, False).start()

    @pl.when(sa == 0)
    def _():
        for g in range(2):
            load(g, True).start()

    pl.semaphore_wait(barrier, len(peers))

    @pl.when(sa == 0)
    def _():
        for d in (1, 2, 3):
            merge_copy(1, d).start()

    row = velocity[...]
    lane = lax.broadcasted_iota(jnp.int32, (1, NY), 1)
    after = pltpu.roll(row, NY - 1, 1)
    before = pltpu.roll(row, 1, 1)
    shear = jnp.where(
        lane == 0, after - row, jnp.where(lane == NY - 1, row - before, (after - before) * 0.5)
    )
    drift_row[...] = row * (0.5 * step_length)
    shear_row[...] = shear * step_length

    def split_into(target, value):
        high = value.astype(jnp.bfloat16)
        low = (value - high.astype(jnp.float32)).astype(jnp.bfloat16)
        target[pl.ds(0, NY), :] = high
        target[pl.ds(NY, NY), :] = high
        target[pl.ds(2 * NY, NY), :] = low

    split_into(solve, wall[...])
    split_into(solve_t, wall[...].T)
    squares[...] = jnp.zeros_like(squares)

    def split_rows(start, value):
        rows = value.shape[0] * value.shape[1]
        flat = value.reshape(rows, NY)
        high = flat.astype(jnp.bfloat16)
        low = (flat - high.astype(jnp.float32)).astype(jnp.bfloat16)
        target = (lhs0, lhs1)[start // HALF]
        place = pl.ds(start % HALF, rows)
        target[place, pl.ds(0, NY)] = high
        target[place, pl.ds(NY, NY)] = low
        target[place, pl.ds(2 * NY, NY)] = high

    def product(weights):
        return [
            jnp.dot(part[...], weights[...], preferred_element_type=jnp.float32)
            for part in (lhs0, lhs1)
        ]

    def halo_copy(e, g, field, merged, k):
        part = pl.ds(*GROUPS[g][:2])
        if k < 4:
            half, way = divmod(k, 2)
            cells = pl.ds(half * (CELLS // 2), CELLS // 2)
            if merged:
                src = edge_out.at[e, way, part, 0, cells]
                dst = edge_in.at[e, 1 - way, part, 0, cells]
                device = y_peer(3) if way else y_peer(1)
            else:
                src = edge_out.at[e, way, part, :, cells]
                dst = edge_in.at[e, 1 - way, part, :, cells]
                device = gz_peer(-1) if way else gz_peer(1)
        elif k == 4:
            src, dst, device = field.at[part, :, CELLS], field.at[part, :, 0], z_peer(1)
        else:
            src, dst, device = field.at[part, :, 1], field.at[part, :, CELLS + 1], z_peer(3)
        return remote(src, dst, send_sem.at[e, g, k], recv_sem.at[e, g, k], device)

    def put_edges(e, c, b, cells, value, merged):
        if not merged:
            edge_out[e, 0, c, b, cells] = value[:, 7:8, :]
            edge_out[e, 1, c, b, cells] = value[:, 0:1, :]
        elif b == BLOCKS - 1:
            edge_out[e, 0, c, 0, cells] = value[:, 7:8, :]
        elif b == 0:
            edge_out[e, 1, c, 0, cells] = value[:, 0:1, :]

    def north_row(e, field, c, b, x0, p0, width, merged):
        if merged and b < BLOCKS - 1:
            return field[c, b + 1, pl.ds(x0 + 1, width), 0:1, :]
        return edge_in[e, 0, c, 0 if merged else b, pl.ds(p0, width)]

    def south_row(e, field, c, b, x0, p0, width, merged):
        if merged and b > 0:
            return field[c, b - 1, pl.ds(x0 + 1, width), 7:8, :]
        return edge_in[e, 1, c, 0 if merged else b, pl.ds(p0, width)]

    def stepped(e, g, field, extra, adjoint, x0, p0, merged):
        c0, nc, width = GROUPS[g]
        drift = drift_row[...].reshape(1, 1, NY)
        shear = shear_row[...].reshape(1, 1, NY)
        if adjoint:
            drift = -drift
        level = lax.broadcasted_iota(jnp.int32, (width, 8, NY), 1)
        out = {}
        for b in range(BLOCKS):
            centers = [field[c, b, pl.ds(x0 + 1, width)] for c in range(c0, c0 + nc)]
            for i in range(nc):
                c = c0 + i
                center = centers[i]
                east = field[c, b, pl.ds(x0 + 2, width)]
                west = field[c, b, pl.ds(x0, width)]
                place = (e, field, c, b, x0, p0, width, merged)
                north = jnp.where(level == 7, north_row(*place), pltpu.roll(center, 7, 1))
                south = jnp.where(level == 0, south_row(*place), pltpu.roll(center, 1, 1))
                value = (step_length * viscosity) * ((east + west) + (north + south))
                value = value + drift * (west - east)
                if extra is None:
                    value = value + (1.0 - 4.0 * step_length * viscosity + step_length) * center
                else:
                    value = value + (1.0 - 4.0 * step_length * viscosity) * center
                    value = value + step_length * extra(c, b, x0, width)
                if nc == 2 and i == (1 if adjoint else 0):
                    value = value - shear * centers[1 - i]
                out[i, b] = value
        return out

    def passes(g, body, merged, source=None, target=None):
        width = GROUPS[g][2]
        count = CELLS // width
        if count == 2:
            needed = {0: (0, 1, 4), 1: (2, 3, 5)}
            made = {0: (0, 1, 5), 1: (2, 3, 4)}
        else:
            needed = {0: (0, 1, 4, 5), 2: (2, 3)}
            made = {1: (0, 1, 4, 5), 3: (2, 3)}

        def one(i, carry):
            if count == 2:
                x0 = i * width
            else:
                x0 = lax.select(i < 2, i * (CELLS - width), (i - 1) * width)
            if source is not None:
                for at, copies in needed.items():

                    @pl.when(i == at)
                    def _(copies=copies):
                        for k in copies:
                            halo_copy(*source, merged, k).wait_recv()

            body(pl.multiple_of(x0, width), pl.multiple_of(i * width, width))
            if target is not None:
                for at, copies in made.items():

                    @pl.when(i == at)
                    def _(copies=copies):
                        for k in copies:
                            halo_copy(*target, merged, k).start()

            return carry

        lax.fori_loop(0, count, one, 0)

    def run_group(g, body, merged, source, target):
        c0, nc, width = GROUPS[g]
        tile = width * 8

        def spread(values):
            for i in range(nc):
                for b in range(BLOCKS):
                    split_rows((i * BLOCKS + b) * tile, values[i, b])

        def solved(weights):
            prod = product(weights)
            out = {}
            for i in range(nc):
                for b in range(BLOCKS):
                    half, first = divmod((i * BLOCKS + b) * tile, HALF)
                    out[i, b] = prod[half][first : first + tile].reshape(width, 8, NY)
            return out

        passes(g, lambda x0, p0: body(x0, p0, spread, solved), merged, source, target)

    def put(e, g, field, values, x0, p0, merged):
        c0, nc, width = GROUPS[g]
        for i in range(nc):
            for b in range(BLOCKS):
                field[c0 + i, b, pl.ds(x0 + 1, width)] = values[i, b]
                put_edges(e, c0 + i, b, pl.ds(p0, width), values[i, b], merged)

    def forcing_at(c, b, x0, width):
        return field0[c, b, pl.ds(x0 + 1, width)]

    def held_at(c, b, x0, width):
        return held[c, b, pl.ds(x0, width)]

    def chain(merged):
        def start(g):
            c0, nc, width = GROUPS[g]
            load(g, merged).wait()
            if merged:
                if g == 1:
                    for d in (1, 2, 3):
                        merge_copy(1, d).wait_send()
                        merge_copy(0, d).start()
                for d in (1, 2, 3):
                    merge_copy(g, d).wait_recv()

            def edges(x0, p0):
                for c in range(c0, c0 + nc):
                    for b in (0, BLOCKS - 1) if merged else range(BLOCKS):
                        value = field0[c, b, pl.ds(x0 + 1, width)]
                        put_edges(0, c, b, pl.ds(p0, width), value, merged)

            passes(g, edges, merged, target=(0, g, field0))

        def first(g):
            def body(x0, p0, spread, solved):
                spread(stepped(0, g, field0, None, False, x0, p0, merged))
                put(1, g, field1, solved(solve), x0, p0, merged)

            run_group(g, body, merged, (0, g, field0), (1, g, field1))

        def second(g):
            c0, nc, width = GROUPS[g]

            def body(x0, p0, spread, solved):
                spread(stepped(1, g, field1, forcing_at, False, x0, p0, merged))
                values = solved(solve)
                for b in range(BLOCKS):
                    total = squares[b]
                    for i in range(nc):
                        value = values[i, b]
                        held[c0 + i, b, pl.ds(x0, width)] = value
                        total = total + jnp.sum(value * value, axis=0)
                    squares[b] = total
                spread(values)
                put(2, g, field2, solved(solve_t), x0, p0, merged)

            run_group(g, body, merged, (1, g, field1), (2, g, field2))

        def third(g):
            def body(x0, p0, spread, solved):
                spread(stepped(2, g, field2, held_at, True, x0, p0, merged))
                put(3, g, field3, solved(solve_t), x0, p0, merged)

            run_group(g, body, merged, (2, g, field2), (3, g, field3))

        def fourth(g):
            c0, nc, width = GROUPS[g]

            def body(x0, p0):
                values = stepped(3, g, field3, held_at, True, x0, p0, merged)
                for i in range(nc):
                    for b in range(BLOCKS):
                        sketch[c0 + i, b, pl.ds(x0, width)] = values[i, b]

            passes(g, body, merged, source=(3, g, field3))

        stages = (start, first, second, third, fourth)
        if merged:
            for stage in stages:
                stage(1)
            give(0)
            give(1)
            for stage in stages[:3]:
                stage(0)
            for stage in stages[3:]:
                stage(0)
            give(2)
        else:
            for stage in stages:
                for g in range(2):
                    stage(g)

    def spread_copy(c, t):
        return remote(
            sketch.at[c, t],
            other.at[c, in_row],
            sketch_send.at[c, t],
            sketch_recv.at[c, in_row],
            (gx, y * 4 + t, 1),
        )

    def near_copy(c):
        return remote(
            sketch.at[c, near],
            other.at[c, in_row],
            near_send.at[c],
            sketch_recv.at[c, in_row],
            (gx, y * 4 + near, 0),
        )

    def relay_copy(c, k):
        return remote(
            other.at[c, k],
            other.at[c, k],
            relay_send.at[c, k],
            sketch_recv.at[c, k],
            (gx, gz, 0),
        )

    def own_copy(c):
        return pltpu.make_async_copy(sketch.at[c, in_row], other.at[c, in_row], own_sem.at[c])

    def sketch_wait(c, k):
        remote(
            other.at[c, k],
            other.at[c, k],
            relay_send.at[c, k],
            sketch_recv.at[c, k],
            (gx, gz, 1 - sa),
        ).wait_recv()

    def store(c):
        return pltpu.make_async_copy(other.at[c], other_out.at[c], store_sem.at[c])

    def store_own(c):
        return pltpu.make_async_copy(sketch.at[c], sketch_out.at[c], store_sem.at[3 + c])

    def give(c, in_turn=False):
        for k in range(2):
            spread_copy(c, far_first + k).start()
            spread_copy(c, near_first + k).start()
            if in_turn and k == 0:
                spread_copy(c, far_first).wait_send()
                spread_copy(c, near_first).wait_send()
        near_copy(c).start()
        own_copy(c).start()

    def given(c):
        for t in range(BLOCKS):
            spread_copy(c, t).wait_send()

    row_id = lax.broadcasted_iota(jnp.int32, (8, 128), 0)
    lane_id = lax.broadcasted_iota(jnp.int32, (8, 128), 1)
    zero = jnp.zeros((8, 128), jnp.float32)

    def place(i, j, acc):
        total = jnp.sum(acc, axis=(0, 1), keepdims=True)
        return jnp.where((row_id == i) & (lane_id == j), total, 0.0)

    def products(c, accs, pairs, sources):
        def one(x, accs):
            accs = list(accs)
            for half in range(2):
                part = pl.ds(half * 128, 128)
                values = [s[c, b, x, :, part] for s in sources for b in range(BLOCKS)]
                for n, (i, j) in enumerate(pairs):
                    accs[n] = accs[n] + values[i] * values[j]
            return tuple(accs)

        return lax.fori_loop(0, CELLS, one, accs)

    @pl.when(sa == 0)
    def _():
        chain(True)
        square = squares[0] + squares[1] + squares[2] + squares[3]
        local_gram[...] = place(in_row, 8, square[:, :128] + square[:, 128:])

    @pl.when(sa == 1)
    def _():
        chain(False)
        for c in range(3):
            store_own(c).start()
        own_pairs = [(i, j) for i in range(BLOCKS) for j in range(i, BLOCKS)]
        accs = tuple(zero for _ in own_pairs)
        for c in range(3):
            accs = products(c, accs, own_pairs, [sketch])
        tile = zero
        for n, (i, j) in enumerate(own_pairs):
            tile = tile + place(i + 4, j + 4, accs[n])
        for b in range(BLOCKS):
            square = squares[b]
            tile = tile + place(b + 4, 8, square[:, :128] + square[:, 128:])
        local_gram[...] = tile
        pairs = [(i, j) for i in range(BLOCKS) for j in range(i, 2 * BLOCKS)]
        accs = tuple(zero for _ in pairs)
        for c in range(3):
            for k in range(2):
                sketch_wait(c, far_first + k)
                relay_copy(c, far_first + k).start()
            for k in range(2):
                sketch_wait(c, near_first + k)
            store(c).start()
            accs = products(c, accs, pairs, [other, sketch])
        tile = zero
        for n, (i, j) in enumerate(pairs):
            tile = tile + place(i, j, accs[n])
        local_gram[...] += tile

    def sums(first_sem, buffer, me, peer, count):
        return [
            remote(
                buffer.at[me],
                buffer.at[me],
                sum_send.at[first_sem + d],
                sum_recv.at[first_sem + d],
                peer(d + 1),
            )
            for d in range(count - 1)
        ]

    def collect():
        for c in range(3):
            own_copy(c).wait()
            for d in (1, 2, 3):
                sketch_wait(c, lax.rem(in_row + d, 4))
            store(c).start()

    total = local_gram[...]
    levels = [
        (0, row_sums, rank, row_peer, 8),
        (7, plane_sums, gx * 4 + y, plane_peer, 16),
    ]
    for first_sem, buffer, me, peer, count in levels:
        buffer[me] = total
        for copy in sums(first_sem, buffer, me, peer, count):
            copy.start()
        for copy in sums(first_sem, buffer, me, peer, count):
            copy.wait_recv()
        total = buffer[0]
        for k in range(1, count):
            total = total + buffer[k]

    pl.when(sa == 0)(collect)

    gram_out[...] = total

    def drain(merged):
        for e, field in enumerate((field0, field1, field2, field3)):
            for g in range(2):
                for k in range(6):
                    halo_copy(e, g, field, merged, k).wait_send()

    @pl.when(sa == 0)
    def _():
        drain(True)
        for d in (1, 2, 3):
            merge_copy(0, d).wait_send()
        given(0)
        given(1)
        given(2)
        for c in range(3):
            near_copy(c).wait_send()

    @pl.when(sa == 1)
    def _():
        for c in range(3):
            store_own(c).wait()
        drain(False)
        for c in range(3):
            for k in range(2):
                relay_copy(c, far_first + k).wait_send()

    for c in range(3):
        store(c).wait()
    for first_sem, buffer, me, peer, count in levels:
        for copy in sums(first_sem, buffer, me, peer, count):
            copy.wait_send()


def basis_kernel(
    entries, low, high, gram, basis, factor_out, splats, coefs, first, second, result, sems
):
    sa = lax.axis_index("sa")

    def load(c, k):
        src, dst = ((low, first), (high, second))[k]
        return pltpu.make_async_copy(src.at[c], dst.at[c], sems.at[3 * k + c])

    def store(c):
        return pltpu.make_async_copy(result.at[c], basis.at[c], sems.at[6 + c])

    for c in range(3):
        load(c, 0).start()

    @pl.when(sa == 1)
    def _():
        for c in range(3):
            load(c, 1).start()

    total = gram[...]
    row_id = lax.broadcasted_iota(jnp.int32, (8, 128), 0)
    lane_id = lax.broadcasted_iota(jnp.int32, (8, 128), 1)
    for j in range(9):
        turned = total if j == 0 else pltpu.roll(total, 128 - j, 1)
        splats[j] = jnp.broadcast_to(turned[:, 0:1], (8, 128))
    scale = [jnp.sqrt(splats[8, i : i + 1] / entries + 1e-06) for i in range(8)]
    rows = []
    for p in range(8):
        current = {
            j: splats[j, p : p + 1] / entries / (scale[p] * scale[j]) for j in range(p, 8)
        }
        for q in range(p):
            current = {j: current[j] - rows[q][p] * rows[q][j] for j in current}
        root = jnp.sqrt(current[p])
        rows.append({j: current[j] / root for j in current})
    inverse = [None] * 8
    for p in range(7, -1, -1):
        current = {
            j: jnp.full((1, 128), 1.0 if j == p else 0.0, jnp.float32) for j in range(p, 8)
        }
        for q in range(p + 1, 8):
            for j in range(q, 8):
                current[j] = current[j] - rows[p][q] * inverse[q][j]
        inverse[p] = {j: current[j] / rows[p][p] for j in current}
    tile = jnp.zeros((8, 128), jnp.float32)
    for i in range(8):
        for j in range(i, 8):
            tile = tile + jnp.where((row_id == i) & (lane_id == j), rows[i][j], 0.0)
            coefs[i, pl.ds(j, 1)] = inverse[i][j] / scale[i]
    factor_out[...] = tile[:, :8]

    def combine(start, sources):
        weights = {
            (i, j): jnp.broadcast_to(coefs[i, pl.ds(start + j, 1)], (8, 128))
            for j in range(BLOCKS)
            for i in range(start + j + 1)
        }
        for c in range(3):
            for k in range(len(sources)):
                load(c, k).wait()

            def one(x, carry):
                for half in range(2):
                    part = pl.ds(half * 128, 128)
                    values = [s[c, b, x, :, part] for s in sources for b in range(BLOCKS)]
                    for j in range(BLOCKS):
                        acc = weights[0, j] * values[0]
                        for i in range(1, start + j + 1):
                            acc = acc + weights[i, j] * values[i]
                        result[c, j, x, :, part] = acc
                return carry

            lax.fori_loop(0, CELLS, one, 0)
            store(c).start()

    @pl.when(sa == 0)
    def _():
        combine(0, [first])

    @pl.when(sa == 1)
    def _():
        combine(4, [first, second])

    for c in range(3):
        store(c).wait()


def shards(forcing, velocity, wall_solve):
    f32, bf16 = jnp.float32, jnp.bfloat16
    entries = (
        3
        * forcing.shape[2]
        * lax.axis_size("gx")
        * forcing.shape[3]
        * lax.axis_size("gz")
        * forcing.shape[4]
    )
    tile = (3, BLOCKS, CELLS, 8, NY)
    padded = (3, BLOCKS, CELLS + 2, 8, NY)
    edges = (4, 2, 3, BLOCKS, CELLS, 1, NY)
    vmem = pl.BlockSpec(memory_space=pltpu.VMEM)
    hbm = pl.BlockSpec(memory_space=pl.ANY)
    array = jax.ShapeDtypeStruct(tile, f32)
    low, high, gram = pl.pallas_call(
        kernel,
        out_shape=(
            array,
            array,
            jax.ShapeDtypeStruct((8, 128), f32),
        ),
        in_specs=[hbm, vmem, vmem],
        out_specs=(hbm, hbm, vmem),
        scratch_shapes=[
            pltpu.VMEM(padded, f32),
            pltpu.VMEM(padded, f32),
            pltpu.VMEM(padded, f32),
            pltpu.VMEM(padded, f32),
            pltpu.VMEM(tile, f32),
            pltpu.VMEM(tile, f32),
            pltpu.VMEM(tile, f32),
            pltpu.VMEM(edges, f32),
            pltpu.VMEM(edges, f32),
            pltpu.VMEM((HALF, 3 * NY), bf16),
            pltpu.VMEM((HALF, 3 * NY), bf16),
            pltpu.VMEM((3 * NY, NY), bf16),
            pltpu.VMEM((3 * NY, NY), bf16),
            pltpu.VMEM((1, NY), f32),
            pltpu.VMEM((1, NY), f32),
            pltpu.VMEM((BLOCKS, 8, NY), f32),
            pltpu.VMEM((8, 128), f32),
            pltpu.VMEM((8, 8, 128), f32),
            pltpu.VMEM((16, 8, 128), f32),
            pltpu.SemaphoreType.DMA((2,)),
            pltpu.SemaphoreType.DMA((2, 3)),
            pltpu.SemaphoreType.DMA((2, 3)),
            pltpu.SemaphoreType.DMA((4, 2, 6)),
            pltpu.SemaphoreType.DMA((4, 2, 6)),
            pltpu.SemaphoreType.DMA((3, 4)),
            pltpu.SemaphoreType.DMA((3, 4)),
            pltpu.SemaphoreType.DMA((3, 4)),
            pltpu.SemaphoreType.DMA((3,)),
            pltpu.SemaphoreType.DMA((3,)),
            pltpu.SemaphoreType.DMA((22,)),
            pltpu.SemaphoreType.DMA((22,)),
            pltpu.SemaphoreType.DMA((6,)),
        ],
        compiler_params=pltpu.CompilerParams(
            collective_id=0, has_side_effects=True, vmem_limit_bytes=56 << 20
        ),
        name="sketch",
    )(forcing, velocity.reshape(1, NY), wall_solve)
    return pl.pallas_call(
        functools.partial(basis_kernel, float(entries)),
        out_shape=(array, jax.ShapeDtypeStruct((8, 8), f32)),
        in_specs=[hbm, hbm, vmem],
        out_specs=(hbm, vmem),
        scratch_shapes=[
            pltpu.VMEM((9, 8, 128), f32),
            pltpu.VMEM((8, 8, 128), f32),
            pltpu.VMEM(tile, f32),
            pltpu.VMEM(tile, f32),
            pltpu.VMEM(tile, f32),
            pltpu.SemaphoreType.DMA((9,)),
        ],
        compiler_params=pltpu.CompilerParams(vmem_limit_bytes=60 << 20),
        name="basis",
    )(low, high, gram)


def solution(mesh):
    return jax.shard_map(
        shards,
        mesh=mesh,
        in_specs=(P(None, "sa", "gx", "gz", None), P(), P()),
        out_specs=(P(None, "sa", "gx", "gz", None), P()),
        check_vma=False,
    )
```

```python
import functools

import jax
import jax.numpy as jnp
from jax import lax
from jax.experimental import pallas as pl
from jax.experimental.pallas import tpu as pltpu
from jax.sharding import PartitionSpec as P

MESH = pl.DeviceIdType.MESH
step_length = 0.4
viscosity = 0.2
GROUPS = ((2, 1, 16), (0, 2, 8))
BLOCKS = 4
CELLS = 32
NY = 256
HALF = 256


def kernel(
    forcing,
    velocity,
    wall,
    other_out,
    sketch_out,
    gram_out,
    field0,
    field1,
    field2,
    field3,
    held,
    sketch,
    other,
    edge_out,
    edge_in,
    lhs0,
    lhs1,
    solve,
    solve_t,
    drift_row,
    shear_row,
    squares,
    local_gram,
    row_sums,
    plane_sums,
    load_sem,
    merge_send,
    merge_recv,
    send_sem,
    recv_sem,
    sketch_send,
    sketch_recv,
    relay_send,
    near_send,
    own_sem,
    sum_send,
    sum_recv,
    store_sem,
):
    gx, gz, sa = lax.axis_index("gx"), lax.axis_index("gz"), lax.axis_index("sa")
    in_row, y = lax.rem(gz, 4), lax.div(gz, 4)
    rank = in_row * 2 + sa

    def row_peer(offset):
        other_rank = lax.rem(rank + offset, 8)
        return (gx, y * 4 + lax.div(other_rank, 2), lax.rem(other_rank, 2))

    def y_peer(offset):
        return (gx, lax.rem(y + offset, 4) * 4 + in_row, sa)

    def z_peer(offset):
        return (lax.rem(gx + offset, 4), gz, sa)

    def plane_peer(offset):
        place = lax.rem(gx * 4 + y + offset, 16)
        return (lax.div(place, 4), lax.rem(place, 4) * 4 + in_row, sa)

    def gz_peer(offset):
        return (gx, lax.rem(gz + offset + 16, 16), sa)

    near = in_row + 1 - 2 * lax.rem(in_row, 2)
    far_first = 2 - 2 * lax.div(in_row, 2)
    near_first = 2 * lax.div(in_row, 2)

    def load(g, merged):
        part = pl.ds(*GROUPS[g][:2])
        if merged:
            return pltpu.make_async_copy(
                forcing.at[part, in_row],
                field0.at[part, in_row, pl.ds(1, CELLS)],
                load_sem.at[g],
            )
        return pltpu.make_async_copy(
            forcing.at[part], field0.at[part, :, pl.ds(1, CELLS)], load_sem.at[g]
        )

    def remote(src, dst, sent, received, device):
        return pltpu.make_async_remote_copy(
            src_ref=src,
            dst_ref=dst,
            send_sem=sent,
            recv_sem=received,
            device_id=device,
            device_id_type=MESH,
        )

    def merge_copy(g, d):
        part = pl.ds(*GROUPS[g][:2])
        column = lax.rem(in_row + d, 4)
        return remote(
            forcing.at[part, column],
            field0.at[part, in_row, pl.ds(1, CELLS)],
            merge_send.at[g, d - 1],
            merge_recv.at[g, d - 1],
            (gx, y * 4 + column, sa),
        )

    barrier = pltpu.get_barrier_semaphore()
    peers = [row_peer(d) for d in range(1, 8)]
    peers += [plane_peer(d) for d in range(1, 16)]
    peers += [gz_peer(1), gz_peer(-1)]
    for peer in peers:
        pl.semaphore_signal(barrier, inc=1, device_id=peer, device_id_type=MESH)

    @pl.when(sa == 1)
    def _():
        for g in range(2):
            load(g, False).start()

    @pl.when(sa == 0)
    def _():
        for g in range(2):
            load(g, True).start()

    pl.semaphore_wait(barrier, len(peers))

    @pl.when(sa == 0)
    def _():
        for d in (1, 2, 3):
            merge_copy(1, d).start()

    row = velocity[...]
    lane = lax.broadcasted_iota(jnp.int32, (1, NY), 1)
    after = pltpu.roll(row, NY - 1, 1)
    before = pltpu.roll(row, 1, 1)
    shear = jnp.where(
        lane == 0, after - row, jnp.where(lane == NY - 1, row - before, (after - before) * 0.5)
    )
    drift_row[...] = row * (0.5 * step_length)
    shear_row[...] = shear * step_length

    def split_into(target, value):
        high = value.astype(jnp.bfloat16)
        low = (value - high.astype(jnp.float32)).astype(jnp.bfloat16)
        target[pl.ds(0, NY), :] = high
        target[pl.ds(NY, NY), :] = high
        target[pl.ds(2 * NY, NY), :] = low

    split_into(solve, wall[...])
    split_into(solve_t, wall[...].T)
    squares[...] = jnp.zeros_like(squares)

    def split_rows(start, value):
        rows = value.shape[0] * value.shape[1]
        flat = value.reshape(rows, NY)
        high = flat.astype(jnp.bfloat16)
        low = (flat - high.astype(jnp.float32)).astype(jnp.bfloat16)
        target = (lhs0, lhs1)[start // HALF]
        place = pl.ds(start % HALF, rows)
        target[place, pl.ds(0, NY)] = high
        target[place, pl.ds(NY, NY)] = low
        target[place, pl.ds(2 * NY, NY)] = high

    def product(weights):
        return [
            jnp.dot(part[...], weights[...], preferred_element_type=jnp.float32)
            for part in (lhs0, lhs1)
        ]

    def halo_copy(e, g, field, merged, k):
        part = pl.ds(*GROUPS[g][:2])
        if k < 4:
            half, way = divmod(k, 2)
            cells = pl.ds(half * (CELLS // 2), CELLS // 2)
            if merged:
                src = edge_out.at[e, way, part, 0, cells]
                dst = edge_in.at[e, 1 - way, part, 0, cells]
                device = y_peer(3) if way else y_peer(1)
            else:
                src = edge_out.at[e, way, part, :, cells]
                dst = edge_in.at[e, 1 - way, part, :, cells]
                device = gz_peer(-1) if way else gz_peer(1)
        elif k == 4:
            src, dst, device = field.at[part, :, CELLS], field.at[part, :, 0], z_peer(1)
        else:
            src, dst, device = field.at[part, :, 1], field.at[part, :, CELLS + 1], z_peer(3)
        return remote(src, dst, send_sem.at[e, g, k], recv_sem.at[e, g, k], device)

    def put_edges(e, c, b, cells, value, merged):
        if not merged:
            edge_out[e, 0, c, b, cells] = value[:, 7:8, :]
            edge_out[e, 1, c, b, cells] = value[:, 0:1, :]
        elif b == BLOCKS - 1:
            edge_out[e, 0, c, 0, cells] = value[:, 7:8, :]
        elif b == 0:
            edge_out[e, 1, c, 0, cells] = value[:, 0:1, :]

    def north_row(e, field, c, b, x0, p0, width, merged):
        if merged and b < BLOCKS - 1:
            return field[c, b + 1, pl.ds(x0 + 1, width), 0:1, :]
        return edge_in[e, 0, c, 0 if merged else b, pl.ds(p0, width)]

    def south_row(e, field, c, b, x0, p0, width, merged):
        if merged and b > 0:
            return field[c, b - 1, pl.ds(x0 + 1, width), 7:8, :]
        return edge_in[e, 1, c, 0 if merged else b, pl.ds(p0, width)]

    def stepped(e, g, field, extra, adjoint, x0, p0, merged):
        c0, nc, width = GROUPS[g]
        drift = drift_row[...].reshape(1, 1, NY)
        shear = shear_row[...].reshape(1, 1, NY)
        if adjoint:
            drift = -drift
        level = lax.broadcasted_iota(jnp.int32, (width, 8, NY), 1)
        out = {}
        for b in range(BLOCKS):
            centers = [field[c, b, pl.ds(x0 + 1, width)] for c in range(c0, c0 + nc)]
            for i in range(nc):
                c = c0 + i
                center = centers[i]
                east = field[c, b, pl.ds(x0 + 2, width)]
                west = field[c, b, pl.ds(x0, width)]
                place = (e, field, c, b, x0, p0, width, merged)
                north = jnp.where(level == 7, north_row(*place), pltpu.roll(center, 7, 1))
                south = jnp.where(level == 0, south_row(*place), pltpu.roll(center, 1, 1))
                value = (step_length * viscosity) * ((east + west) + (north + south))
                value = value + drift * (west - east)
                if extra is None:
                    value = value + (1.0 - 4.0 * step_length * viscosity + step_length) * center
                else:
                    value = value + (1.0 - 4.0 * step_length * viscosity) * center
                    value = value + step_length * extra(c, b, x0, width)
                if nc == 2 and i == (1 if adjoint else 0):
                    value = value - shear * centers[1 - i]
                out[i, b] = value
        return out

    def passes(g, body, merged, source=None, target=None):
        width = GROUPS[g][2]
        count = CELLS // width
        if count == 2:
            needed = {0: (0, 1, 4), 1: (2, 3, 5)}
            made = {0: (0, 1, 5), 1: (2, 3, 4)}
        else:
            needed = {0: (0, 1, 4, 5), 2: (2, 3)}
            made = {1: (0, 1, 4, 5), 3: (2, 3)}

        def one(i, carry):
            if count == 2:
                x0 = i * width
            else:
                x0 = lax.select(i < 2, i * (CELLS - width), (i - 1) * width)
            if source is not None:
                for at, copies in needed.items():

                    @pl.when(i == at)
                    def _(copies=copies):
                        for k in copies:
                            halo_copy(*source, merged, k).wait_recv()

            body(pl.multiple_of(x0, width), pl.multiple_of(i * width, width))
            if target is not None:
                for at, copies in made.items():

                    @pl.when(i == at)
                    def _(copies=copies):
                        for k in copies:
                            halo_copy(*target, merged, k).start()

            return carry

        lax.fori_loop(0, count, one, 0)

    def run_group(g, body, merged, source, target):
        c0, nc, width = GROUPS[g]
        tile = width * 8

        def spread(values):
            for i in range(nc):
                for b in range(BLOCKS):
                    split_rows((i * BLOCKS + b) * tile, values[i, b])

        def solved(weights):
            prod = product(weights)
            out = {}
            for i in range(nc):
                for b in range(BLOCKS):
                    half, first = divmod((i * BLOCKS + b) * tile, HALF)
                    out[i, b] = prod[half][first : first + tile].reshape(width, 8, NY)
            return out

        passes(g, lambda x0, p0: body(x0, p0, spread, solved), merged, source, target)

    def put(e, g, field, values, x0, p0, merged):
        c0, nc, width = GROUPS[g]
        for i in range(nc):
            for b in range(BLOCKS):
                field[c0 + i, b, pl.ds(x0 + 1, width)] = values[i, b]
                put_edges(e, c0 + i, b, pl.ds(p0, width), values[i, b], merged)

    def forcing_at(c, b, x0, width):
        return field0[c, b, pl.ds(x0 + 1, width)]

    def held_at(c, b, x0, width):
        return held[c, b, pl.ds(x0, width)]

    def chain(merged):
        def start(g):
            c0, nc, width = GROUPS[g]
            load(g, merged).wait()
            if merged:
                if g == 1:
                    for d in (1, 2, 3):
                        merge_copy(1, d).wait_send()
                        merge_copy(0, d).start()
                for d in (1, 2, 3):
                    merge_copy(g, d).wait_recv()

            def edges(x0, p0):
                for c in range(c0, c0 + nc):
                    for b in (0, BLOCKS - 1) if merged else range(BLOCKS):
                        value = field0[c, b, pl.ds(x0 + 1, width)]
                        put_edges(0, c, b, pl.ds(p0, width), value, merged)

            passes(g, edges, merged, target=(0, g, field0))

        def first(g):
            def body(x0, p0, spread, solved):
                spread(stepped(0, g, field0, None, False, x0, p0, merged))
                put(1, g, field1, solved(solve), x0, p0, merged)

            run_group(g, body, merged, (0, g, field0), (1, g, field1))

        def second(g):
            c0, nc, width = GROUPS[g]

            def body(x0, p0, spread, solved):
                spread(stepped(1, g, field1, forcing_at, False, x0, p0, merged))
                values = solved(solve)
                for b in range(BLOCKS):
                    total = squares[b]
                    for i in range(nc):
                        value = values[i, b]
                        held[c0 + i, b, pl.ds(x0, width)] = value
                        total = total + jnp.sum(value * value, axis=0)
                    squares[b] = total
                spread(values)
                put(2, g, field2, solved(solve_t), x0, p0, merged)

            run_group(g, body, merged, (1, g, field1), (2, g, field2))

        def third(g):
            def body(x0, p0, spread, solved):
                spread(stepped(2, g, field2, held_at, True, x0, p0, merged))
                put(3, g, field3, solved(solve_t), x0, p0, merged)

            run_group(g, body, merged, (2, g, field2), (3, g, field3))

        def fourth(g):
            c0, nc, width = GROUPS[g]

            def body(x0, p0):
                values = stepped(3, g, field3, held_at, True, x0, p0, merged)
                for i in range(nc):
                    for b in range(BLOCKS):
                        sketch[c0 + i, b, pl.ds(x0, width)] = values[i, b]

            passes(g, body, merged, source=(3, g, field3))

        stages = (start, first, second, third, fourth)
        if merged:
            for stage in stages:
                stage(1)
            give(0)
            give(1)
            for stage in stages[:3]:
                stage(0)
            for stage in stages[3:]:
                stage(0)
            give(2)
        else:
            for stage in stages:
                for g in (1, 0):
                    stage(g)

    def spread_copy(c, t):
        return remote(
            sketch.at[c, t],
            other.at[c, in_row],
            sketch_send.at[c, t],
            sketch_recv.at[c, in_row],
            (gx, y * 4 + t, 1),
        )

    def near_copy(c):
        return remote(
            sketch.at[c, near],
            other.at[c, in_row],
            near_send.at[c],
            sketch_recv.at[c, in_row],
            (gx, y * 4 + near, 0),
        )

    def relay_copy(c, k):
        return remote(
            other.at[c, k],
            other.at[c, k],
            relay_send.at[c, k],
            sketch_recv.at[c, k],
            (gx, gz, 0),
        )

    def own_copy(c):
        return pltpu.make_async_copy(sketch.at[c, in_row], other.at[c, in_row], own_sem.at[c])

    def sketch_wait(c, k):
        remote(
            other.at[c, k],
            other.at[c, k],
            relay_send.at[c, k],
            sketch_recv.at[c, k],
            (gx, gz, 1 - sa),
        ).wait_recv()

    def store(c):
        return pltpu.make_async_copy(other.at[c], other_out.at[c], store_sem.at[c])

    def store_own(c):
        return pltpu.make_async_copy(sketch.at[c], sketch_out.at[c], store_sem.at[3 + c])

    def give(c, in_turn=False):
        for k in range(2):
            spread_copy(c, far_first + k).start()
            spread_copy(c, near_first + k).start()
            if in_turn and k == 0:
                spread_copy(c, far_first).wait_send()
                spread_copy(c, near_first).wait_send()
        near_copy(c).start()
        own_copy(c).start()

    def given(c):
        for t in range(BLOCKS):
            spread_copy(c, t).wait_send()

    row_id = lax.broadcasted_iota(jnp.int32, (8, 128), 0)
    lane_id = lax.broadcasted_iota(jnp.int32, (8, 128), 1)
    zero = jnp.zeros((8, 128), jnp.float32)

    def place(i, j, acc):
        total = jnp.sum(acc, axis=(0, 1), keepdims=True)
        return jnp.where((row_id == i) & (lane_id == j), total, 0.0)

    def products(c, accs, pairs, sources):
        def one(x, accs):
            accs = list(accs)
            for half in range(2):
                part = pl.ds(half * 128, 128)
                values = [s[c, b, x, :, part] for s in sources for b in range(BLOCKS)]
                for n, (i, j) in enumerate(pairs):
                    accs[n] = accs[n] + values[i] * values[j]
            return tuple(accs)

        return lax.fori_loop(0, CELLS, one, accs)

    @pl.when(sa == 0)
    def _():
        chain(True)
        square = squares[0] + squares[1] + squares[2] + squares[3]
        local_gram[...] = place(in_row, 8, square[:, :128] + square[:, 128:])

    @pl.when(sa == 1)
    def _():
        chain(False)
        for c in range(3):
            store_own(c).start()
        own_pairs = [(i, j) for i in range(BLOCKS) for j in range(i, BLOCKS)]
        pairs = [(i, j) for i in range(BLOCKS) for j in range(i, 2 * BLOCKS)]
        own_accs = tuple(zero for _ in own_pairs)
        accs = tuple(zero for _ in pairs)
        for c in range(3):
            for k in range(2):
                sketch_wait(c, far_first + k)
                relay_copy(c, far_first + k).start()
            own_accs = products(c, own_accs, own_pairs, [sketch])
            if c == 2:
                tile = zero
                for n, (i, j) in enumerate(own_pairs):
                    tile = tile + place(i + 4, j + 4, own_accs[n])
                for b in range(BLOCKS):
                    square = squares[b]
                    tile = tile + place(b + 4, 8, square[:, :128] + square[:, 128:])
                local_gram[...] = tile
            for k in range(2):
                sketch_wait(c, near_first + k)
            store(c).start()
            accs = products(c, accs, pairs, [other, sketch])
        tile = zero
        for n, (i, j) in enumerate(pairs):
            tile = tile + place(i, j, accs[n])
        local_gram[...] += tile

    def sums(first_sem, buffer, me, peer, count):
        return [
            remote(
                buffer.at[me],
                buffer.at[me],
                sum_send.at[first_sem + d],
                sum_recv.at[first_sem + d],
                peer(d + 1),
            )
            for d in range(count - 1)
        ]

    def collect():
        for c in range(3):
            own_copy(c).wait()
            for d in (1, 2, 3):
                sketch_wait(c, lax.rem(in_row + d, 4))
            store(c).start()

    total = local_gram[...]
    levels = [
        (0, row_sums, rank, row_peer, 8),
        (7, plane_sums, gx * 4 + y, plane_peer, 16),
    ]
    for first_sem, buffer, me, peer, count in levels:
        buffer[me] = total
        for copy in sums(first_sem, buffer, me, peer, count):
            copy.start()
        for copy in sums(first_sem, buffer, me, peer, count):
            copy.wait_recv()
        total = buffer[0]
        for k in range(1, count):
            total = total + buffer[k]

    pl.when(sa == 0)(collect)

    gram_out[...] = total

    def drain(merged):
        for e, field in enumerate((field0, field1, field2, field3)):
            for g in range(2):
                for k in range(6):
                    halo_copy(e, g, field, merged, k).wait_send()

    @pl.when(sa == 0)
    def _():
        drain(True)
        for d in (1, 2, 3):
            merge_copy(0, d).wait_send()
        given(0)
        given(1)
        given(2)
        for c in range(3):
            near_copy(c).wait_send()

    @pl.when(sa == 1)
    def _():
        for c in range(3):
            store_own(c).wait()
        drain(False)
        for c in range(3):
            for k in range(2):
                relay_copy(c, far_first + k).wait_send()

    for c in range(3):
        store(c).wait()
    for first_sem, buffer, me, peer, count in levels:
        for copy in sums(first_sem, buffer, me, peer, count):
            copy.wait_send()


def basis_kernel(
    entries, low, high, gram, basis, factor_out, splats, coefs, first, second, result, sems
):
    sa = lax.axis_index("sa")

    def load(c, k):
        src, dst = ((low, first), (high, second))[k]
        return pltpu.make_async_copy(src.at[c], dst.at[c], sems.at[3 * k + c])

    def store(c):
        return pltpu.make_async_copy(result.at[c], basis.at[c], sems.at[6 + c])

    for c in range(3):
        load(c, 0).start()

    @pl.when(sa == 1)
    def _():
        for c in range(3):
            load(c, 1).start()

    total = gram[...]
    row_id = lax.broadcasted_iota(jnp.int32, (8, 128), 0)
    lane_id = lax.broadcasted_iota(jnp.int32, (8, 128), 1)
    for j in range(9):
        turned = total if j == 0 else pltpu.roll(total, 128 - j, 1)
        splats[j] = jnp.broadcast_to(turned[:, 0:1], (8, 128))
    scale = [jnp.sqrt(splats[8, i : i + 1] / entries + 1e-06) for i in range(8)]
    rows = []
    for p in range(8):
        current = {
            j: splats[j, p : p + 1] / entries / (scale[p] * scale[j]) for j in range(p, 8)
        }
        for q in range(p):
            current = {j: current[j] - rows[q][p] * rows[q][j] for j in current}
        root = jnp.sqrt(current[p])
        rows.append({j: current[j] / root for j in current})
    inverse = [None] * 8
    for p in range(7, -1, -1):
        current = {
            j: jnp.full((1, 128), 1.0 if j == p else 0.0, jnp.float32) for j in range(p, 8)
        }
        for q in range(p + 1, 8):
            for j in range(q, 8):
                current[j] = current[j] - rows[p][q] * inverse[q][j]
        inverse[p] = {j: current[j] / rows[p][p] for j in current}
    tile = jnp.zeros((8, 128), jnp.float32)
    for i in range(8):
        for j in range(i, 8):
            tile = tile + jnp.where((row_id == i) & (lane_id == j), rows[i][j], 0.0)
            coefs[i, pl.ds(j, 1)] = inverse[i][j] / scale[i]
    factor_out[...] = tile[:, :8]

    def combine(start, sources):
        weights = {
            (i, j): jnp.broadcast_to(coefs[i, pl.ds(start + j, 1)], (8, 128))
            for j in range(BLOCKS)
            for i in range(start + j + 1)
        }
        for c in range(3):
            for k in range(len(sources)):
                load(c, k).wait()

            def one(x, carry):
                for half in range(2):
                    part = pl.ds(half * 128, 128)
                    values = [s[c, b, x, :, part] for s in sources for b in range(BLOCKS)]
                    for j in range(BLOCKS):
                        acc = weights[0, j] * values[0]
                        for i in range(1, start + j + 1):
                            acc = acc + weights[i, j] * values[i]
                        result[c, j, x, :, part] = acc
                return carry

            lax.fori_loop(0, CELLS, one, 0)
            store(c).start()

    @pl.when(sa == 0)
    def _():
        combine(0, [first])

    @pl.when(sa == 1)
    def _():
        combine(4, [first, second])

    for c in range(3):
        store(c).wait()


def shards(forcing, velocity, wall_solve):
    f32, bf16 = jnp.float32, jnp.bfloat16
    entries = (
        3
        * forcing.shape[2]
        * lax.axis_size("gx")
        * forcing.shape[3]
        * lax.axis_size("gz")
        * forcing.shape[4]
    )
    tile = (3, BLOCKS, CELLS, 8, NY)
    padded = (3, BLOCKS, CELLS + 2, 8, NY)
    edges = (4, 2, 3, BLOCKS, CELLS, 1, NY)
    vmem = pl.BlockSpec(memory_space=pltpu.VMEM)
    hbm = pl.BlockSpec(memory_space=pl.ANY)
    array = jax.ShapeDtypeStruct(tile, f32)
    low, high, gram = pl.pallas_call(
        kernel,
        out_shape=(
            array,
            array,
            jax.ShapeDtypeStruct((8, 128), f32),
        ),
        in_specs=[hbm, vmem, vmem],
        out_specs=(hbm, hbm, vmem),
        scratch_shapes=[
            pltpu.VMEM(padded, f32),
            pltpu.VMEM(padded, f32),
            pltpu.VMEM(padded, f32),
            pltpu.VMEM(padded, f32),
            pltpu.VMEM(tile, f32),
            pltpu.VMEM(tile, f32),
            pltpu.VMEM(tile, f32),
            pltpu.VMEM(edges, f32),
            pltpu.VMEM(edges, f32),
            pltpu.VMEM((HALF, 3 * NY), bf16),
            pltpu.VMEM((HALF, 3 * NY), bf16),
            pltpu.VMEM((3 * NY, NY), bf16),
            pltpu.VMEM((3 * NY, NY), bf16),
            pltpu.VMEM((1, NY), f32),
            pltpu.VMEM((1, NY), f32),
            pltpu.VMEM((BLOCKS, 8, NY), f32),
            pltpu.VMEM((8, 128), f32),
            pltpu.VMEM((8, 8, 128), f32),
            pltpu.VMEM((16, 8, 128), f32),
            pltpu.SemaphoreType.DMA((2,)),
            pltpu.SemaphoreType.DMA((2, 3)),
            pltpu.SemaphoreType.DMA((2, 3)),
            pltpu.SemaphoreType.DMA((4, 2, 6)),
            pltpu.SemaphoreType.DMA((4, 2, 6)),
            pltpu.SemaphoreType.DMA((3, 4)),
            pltpu.SemaphoreType.DMA((3, 4)),
            pltpu.SemaphoreType.DMA((3, 4)),
            pltpu.SemaphoreType.DMA((3,)),
            pltpu.SemaphoreType.DMA((3,)),
            pltpu.SemaphoreType.DMA((22,)),
            pltpu.SemaphoreType.DMA((22,)),
            pltpu.SemaphoreType.DMA((6,)),
        ],
        compiler_params=pltpu.CompilerParams(
            collective_id=0, has_side_effects=True, vmem_limit_bytes=56 << 20
        ),
        name="sketch",
    )(forcing, velocity.reshape(1, NY), wall_solve)
    return pl.pallas_call(
        functools.partial(basis_kernel, float(entries)),
        out_shape=(array, jax.ShapeDtypeStruct((8, 8), f32)),
        in_specs=[hbm, hbm, vmem],
        out_specs=(hbm, vmem),
        scratch_shapes=[
            pltpu.VMEM((9, 8, 128), f32),
            pltpu.VMEM((8, 8, 128), f32),
            pltpu.VMEM(tile, f32),
            pltpu.VMEM(tile, f32),
            pltpu.VMEM(tile, f32),
            pltpu.SemaphoreType.DMA((9,)),
        ],
        compiler_params=pltpu.CompilerParams(vmem_limit_bytes=60 << 20),
        name="basis",
    )(low, high, gram)


def solution(mesh):
    return jax.shard_map(
        shards,
        mesh=mesh,
        in_specs=(P(None, "sa", "gx", "gz", None), P(), P()),
        out_specs=(P(None, "sa", "gx", "gz", None), P()),
        check_vma=False,
    )
```

```python
import functools

import jax
import jax.numpy as jnp
from jax import lax
from jax.experimental import pallas as pl
from jax.experimental.pallas import tpu as pltpu
from jax.sharding import PartitionSpec as P

MESH = pl.DeviceIdType.MESH
step_length = 0.4
viscosity = 0.2
GROUPS = ((2, 1, 16), (0, 2, 8))
BLOCKS = 4
CELLS = 32
NY = 256
PIECE = 128


def kernel(
    forcing,
    velocity,
    wall,
    other_out,
    sketch_out,
    gram_out,
    field0,
    field1,
    field2,
    field3,
    held,
    sketch,
    other,
    edge_out,
    edge_in,
    lhs0,
    lhs1,
    lhs2,
    lhs3,
    solve,
    solve_t,
    drift_row,
    shear_row,
    squares,
    local_gram,
    row_sums,
    plane_sums,
    load_sem,
    merge_send,
    merge_recv,
    send_sem,
    recv_sem,
    sketch_send,
    sketch_recv,
    relay_send,
    near_send,
    own_sem,
    sum_send,
    sum_recv,
    store_sem,
):
    gx, gz, sa = lax.axis_index("gx"), lax.axis_index("gz"), lax.axis_index("sa")
    in_row, y = lax.rem(gz, 4), lax.div(gz, 4)
    rank = in_row * 2 + sa

    def row_peer(offset):
        other_rank = lax.rem(rank + offset, 8)
        return (gx, y * 4 + lax.div(other_rank, 2), lax.rem(other_rank, 2))

    def y_peer(offset):
        return (gx, lax.rem(y + offset, 4) * 4 + in_row, sa)

    def z_peer(offset):
        return (lax.rem(gx + offset, 4), gz, sa)

    def plane_peer(offset):
        place = lax.rem(gx * 4 + y + offset, 16)
        return (lax.div(place, 4), lax.rem(place, 4) * 4 + in_row, sa)

    def gz_peer(offset):
        return (gx, lax.rem(gz + offset + 16, 16), sa)

    near = in_row + 1 - 2 * lax.rem(in_row, 2)
    far_first = 2 - 2 * lax.div(in_row, 2)
    near_first = 2 * lax.div(in_row, 2)

    def load(g, merged):
        part = pl.ds(*GROUPS[g][:2])
        if merged:
            return pltpu.make_async_copy(
                forcing.at[part, in_row],
                field0.at[part, in_row, pl.ds(1, CELLS)],
                load_sem.at[g],
            )
        return pltpu.make_async_copy(
            forcing.at[part], field0.at[part, :, pl.ds(1, CELLS)], load_sem.at[g]
        )

    def remote(src, dst, sent, received, device):
        return pltpu.make_async_remote_copy(
            src_ref=src,
            dst_ref=dst,
            send_sem=sent,
            recv_sem=received,
            device_id=device,
            device_id_type=MESH,
        )

    def merge_copy(g, d):
        part = pl.ds(*GROUPS[g][:2])
        column = lax.rem(in_row + d, 4)
        return remote(
            forcing.at[part, column],
            field0.at[part, in_row, pl.ds(1, CELLS)],
            merge_send.at[g, d - 1],
            merge_recv.at[g, d - 1],
            (gx, y * 4 + column, sa),
        )

    barrier = pltpu.get_barrier_semaphore()
    peers = [row_peer(d) for d in range(1, 8)]
    peers += [plane_peer(d) for d in range(1, 16)]
    peers += [gz_peer(1), gz_peer(-1)]
    for peer in peers:
        pl.semaphore_signal(barrier, inc=1, device_id=peer, device_id_type=MESH)

    @pl.when(sa == 1)
    def _():
        for g in range(2):
            load(g, False).start()

    @pl.when(sa == 0)
    def _():
        for g in range(2):
            load(g, True).start()

    pl.semaphore_wait(barrier, len(peers))

    @pl.when(sa == 0)
    def _():
        for d in (1, 2, 3):
            merge_copy(1, d).start()

    row = velocity[...]
    lane = lax.broadcasted_iota(jnp.int32, (1, NY), 1)
    after = pltpu.roll(row, NY - 1, 1)
    before = pltpu.roll(row, 1, 1)
    shear = jnp.where(
        lane == 0, after - row, jnp.where(lane == NY - 1, row - before, (after - before) * 0.5)
    )
    drift_row[...] = row * (0.5 * step_length)
    shear_row[...] = shear * step_length

    def split_into(target, value):
        high = value.astype(jnp.bfloat16)
        low = (value - high.astype(jnp.float32)).astype(jnp.bfloat16)
        target[pl.ds(0, NY), :] = high
        target[pl.ds(NY, NY), :] = high
        target[pl.ds(2 * NY, NY), :] = low

    split_into(solve, wall[...])
    split_into(solve_t, wall[...].T)
    squares[...] = jnp.zeros_like(squares)

    def split_rows(start, value):
        rows = value.shape[0] * value.shape[1]
        flat = value.reshape(rows, NY)
        high = flat.astype(jnp.bfloat16)
        low = (flat - high.astype(jnp.float32)).astype(jnp.bfloat16)
        target = (lhs0, lhs1, lhs2, lhs3)[start // PIECE]
        place = pl.ds(start % PIECE, rows)
        target[place, pl.ds(0, NY)] = high
        target[place, pl.ds(NY, NY)] = low
        target[place, pl.ds(2 * NY, NY)] = high

    def product(weights):
        return [
            jnp.dot(part[...], weights[...], preferred_element_type=jnp.float32)
            for part in (lhs0, lhs1, lhs2, lhs3)
        ]

    def halo_copy(e, g, field, merged, k):
        part = pl.ds(*GROUPS[g][:2])
        if k < 4:
            half, way = divmod(k, 2)
            cells = pl.ds(half * (CELLS // 2), CELLS // 2)
            if merged:
                src = edge_out.at[e, way, part, 0, cells]
                dst = edge_in.at[e, 1 - way, part, 0, cells]
                device = y_peer(3) if way else y_peer(1)
            else:
                src = edge_out.at[e, way, part, :, cells]
                dst = edge_in.at[e, 1 - way, part, :, cells]
                device = gz_peer(-1) if way else gz_peer(1)
        elif k == 4:
            src, dst, device = field.at[part, :, CELLS], field.at[part, :, 0], z_peer(1)
        else:
            src, dst, device = field.at[part, :, 1], field.at[part, :, CELLS + 1], z_peer(3)
        return remote(src, dst, send_sem.at[e, g, k], recv_sem.at[e, g, k], device)

    def put_edges(e, c, b, cells, value, merged):
        if not merged:
            edge_out[e, 0, c, b, cells] = value[:, 7:8, :]
            edge_out[e, 1, c, b, cells] = value[:, 0:1, :]
        elif b == BLOCKS - 1:
            edge_out[e, 0, c, 0, cells] = value[:, 7:8, :]
        elif b == 0:
            edge_out[e, 1, c, 0, cells] = value[:, 0:1, :]

    def north_row(e, field, c, b, x0, p0, width, merged):
        if merged and b < BLOCKS - 1:
            return field[c, b + 1, pl.ds(x0 + 1, width), 0:1, :]
        return edge_in[e, 0, c, 0 if merged else b, pl.ds(p0, width)]

    def south_row(e, field, c, b, x0, p0, width, merged):
        if merged and b > 0:
            return field[c, b - 1, pl.ds(x0 + 1, width), 7:8, :]
        return edge_in[e, 1, c, 0 if merged else b, pl.ds(p0, width)]

    def stepped(e, g, field, extra, adjoint, x0, p0, merged):
        c0, nc, width = GROUPS[g]
        drift = drift_row[...].reshape(1, 1, NY)
        shear = shear_row[...].reshape(1, 1, NY)
        if adjoint:
            drift = -drift
        level = lax.broadcasted_iota(jnp.int32, (width, 8, NY), 1)
        out = {}
        for b in range(BLOCKS):
            centers = [field[c, b, pl.ds(x0 + 1, width)] for c in range(c0, c0 + nc)]
            for i in range(nc):
                c = c0 + i
                center = centers[i]
                east = field[c, b, pl.ds(x0 + 2, width)]
                west = field[c, b, pl.ds(x0, width)]
                place = (e, field, c, b, x0, p0, width, merged)
                north = jnp.where(level == 7, north_row(*place), pltpu.roll(center, 7, 1))
                south = jnp.where(level == 0, south_row(*place), pltpu.roll(center, 1, 1))
                value = (step_length * viscosity) * ((east + west) + (north + south))
                value = value + drift * (west - east)
                if extra is None:
                    value = value + (1.0 - 4.0 * step_length * viscosity + step_length) * center
                else:
                    value = value + (1.0 - 4.0 * step_length * viscosity) * center
                    value = value + step_length * extra(c, b, x0, width)
                if nc == 2 and i == (1 if adjoint else 0):
                    value = value - shear * centers[1 - i]
                out[i, b] = value
        return out

    def passes(g, body, merged, source=None, target=None):
        width = GROUPS[g][2]
        count = CELLS // width
        if count == 2:
            needed = {0: (0, 1, 4), 1: (2, 3, 5)}
            made = {0: (0, 1, 5), 1: (2, 3, 4)}
        else:
            needed = {0: (0, 1, 4, 5), 2: (2, 3)}
            made = {1: (0, 1, 4, 5), 3: (2, 3)}

        def one(i, carry):
            if count == 2:
                x0 = i * width
            else:
                x0 = lax.select(i < 2, i * (CELLS - width), (i - 1) * width)
            if source is not None:
                for at, copies in needed.items():

                    @pl.when(i == at)
                    def _(copies=copies):
                        for k in copies:
                            halo_copy(*source, merged, k).wait_recv()

            body(pl.multiple_of(x0, width), pl.multiple_of(i * width, width))
            if target is not None:
                for at, copies in made.items():

                    @pl.when(i == at)
                    def _(copies=copies):
                        for k in copies:
                            halo_copy(*target, merged, k).start()

            return carry

        lax.fori_loop(0, count, one, 0)

    def run_group(g, body, merged, source, target):
        c0, nc, width = GROUPS[g]
        tile = width * 8

        def spread(values):
            for i in range(nc):
                for b in range(BLOCKS):
                    split_rows((i * BLOCKS + b) * tile, values[i, b])

        def solved(weights):
            prod = product(weights)
            out = {}
            for i in range(nc):
                for b in range(BLOCKS):
                    half, first = divmod((i * BLOCKS + b) * tile, PIECE)
                    out[i, b] = prod[half][first : first + tile].reshape(width, 8, NY)
            return out

        passes(g, lambda x0, p0: body(x0, p0, spread, solved), merged, source, target)

    def put(e, g, field, values, x0, p0, merged):
        c0, nc, width = GROUPS[g]
        for i in range(nc):
            for b in range(BLOCKS):
                field[c0 + i, b, pl.ds(x0 + 1, width)] = values[i, b]
                put_edges(e, c0 + i, b, pl.ds(p0, width), values[i, b], merged)

    def forcing_at(c, b, x0, width):
        return field0[c, b, pl.ds(x0 + 1, width)]

    def held_at(c, b, x0, width):
        return held[c, b, pl.ds(x0, width)]

    def chain(merged):
        def start(g):
            c0, nc, width = GROUPS[g]
            load(g, merged).wait()
            if merged:
                if g == 1:
                    for d in (1, 2, 3):
                        merge_copy(1, d).wait_send()
                        merge_copy(0, d).start()
                for d in (1, 2, 3):
                    merge_copy(g, d).wait_recv()

            def edges(x0, p0):
                for c in range(c0, c0 + nc):
                    for b in (0, BLOCKS - 1) if merged else range(BLOCKS):
                        value = field0[c, b, pl.ds(x0 + 1, width)]
                        put_edges(0, c, b, pl.ds(p0, width), value, merged)

            passes(g, edges, merged, target=(0, g, field0))

        def first(g):
            def body(x0, p0, spread, solved):
                spread(stepped(0, g, field0, None, False, x0, p0, merged))
                put(1, g, field1, solved(solve), x0, p0, merged)

            run_group(g, body, merged, (0, g, field0), (1, g, field1))

        def second(g):
            c0, nc, width = GROUPS[g]

            def body(x0, p0, spread, solved):
                spread(stepped(1, g, field1, forcing_at, False, x0, p0, merged))
                values = solved(solve)
                for b in range(BLOCKS):
                    total = squares[b]
                    for i in range(nc):
                        value = values[i, b]
                        held[c0 + i, b, pl.ds(x0, width)] = value
                        total = total + jnp.sum(value * value, axis=0)
                    squares[b] = total
                spread(values)
                put(2, g, field2, solved(solve_t), x0, p0, merged)

            run_group(g, body, merged, (1, g, field1), (2, g, field2))

        def third(g):
            def body(x0, p0, spread, solved):
                spread(stepped(2, g, field2, held_at, True, x0, p0, merged))
                put(3, g, field3, solved(solve_t), x0, p0, merged)

            run_group(g, body, merged, (2, g, field2), (3, g, field3))

        def fourth(g):
            c0, nc, width = GROUPS[g]

            def body(x0, p0):
                values = stepped(3, g, field3, held_at, True, x0, p0, merged)
                for i in range(nc):
                    for b in range(BLOCKS):
                        sketch[c0 + i, b, pl.ds(x0, width)] = values[i, b]

            passes(g, body, merged, source=(3, g, field3))

        stages = (start, first, second, third, fourth)
        if merged:
            for stage in stages:
                stage(1)
            give(0)
            give(1)
            for stage in stages[:3]:
                stage(0)
            for stage in stages[3:]:
                stage(0)
            give(2)
        else:
            for stage in stages:
                for g in range(2):
                    stage(g)

    def spread_copy(c, t):
        return remote(
            sketch.at[c, t],
            other.at[c, in_row],
            sketch_send.at[c, t],
            sketch_recv.at[c, in_row],
            (gx, y * 4 + t, 1),
        )

    def near_copy(c):
        return remote(
            sketch.at[c, near],
            other.at[c, in_row],
            near_send.at[c],
            sketch_recv.at[c, in_row],
            (gx, y * 4 + near, 0),
        )

    def relay_copy(c, k):
        return remote(
            other.at[c, k],
            other.at[c, k],
            relay_send.at[c, k],
            sketch_recv.at[c, k],
            (gx, gz, 0),
        )

    def own_copy(c):
        return pltpu.make_async_copy(sketch.at[c, in_row], other.at[c, in_row], own_sem.at[c])

    def sketch_wait(c, k):
        remote(
            other.at[c, k],
            other.at[c, k],
            relay_send.at[c, k],
            sketch_recv.at[c, k],
            (gx, gz, 1 - sa),
        ).wait_recv()

    def store(c):
        return pltpu.make_async_copy(other.at[c], other_out.at[c], store_sem.at[c])

    def store_own(c):
        return pltpu.make_async_copy(sketch.at[c], sketch_out.at[c], store_sem.at[3 + c])

    def give(c, in_turn=False):
        for k in range(2):
            spread_copy(c, far_first + k).start()
            spread_copy(c, near_first + k).start()
            if in_turn and k == 0:
                spread_copy(c, far_first).wait_send()
                spread_copy(c, near_first).wait_send()
        near_copy(c).start()
        own_copy(c).start()

    def given(c):
        for t in range(BLOCKS):
            spread_copy(c, t).wait_send()

    row_id = lax.broadcasted_iota(jnp.int32, (8, 128), 0)
    lane_id = lax.broadcasted_iota(jnp.int32, (8, 128), 1)
    zero = jnp.zeros((8, 128), jnp.float32)

    def place(i, j, acc):
        total = jnp.sum(acc, axis=(0, 1), keepdims=True)
        return jnp.where((row_id == i) & (lane_id == j), total, 0.0)

    def products(c, accs, pairs, sources):
        def one(x, accs):
            accs = list(accs)
            for half in range(2):
                part = pl.ds(half * 128, 128)
                values = [s[c, b, x, :, part] for s in sources for b in range(BLOCKS)]
                for n, (i, j) in enumerate(pairs):
                    accs[n] = accs[n] + values[i] * values[j]
            return tuple(accs)

        return lax.fori_loop(0, CELLS, one, accs)

    @pl.when(sa == 0)
    def _():
        chain(True)
        square = squares[0] + squares[1] + squares[2] + squares[3]
        local_gram[...] = place(in_row, 8, square[:, :128] + square[:, 128:])

    @pl.when(sa == 1)
    def _():
        chain(False)
        for c in range(3):
            store_own(c).start()
        own_pairs = [(i, j) for i in range(BLOCKS) for j in range(i, BLOCKS)]
        accs = tuple(zero for _ in own_pairs)
        for c in range(3):
            accs = products(c, accs, own_pairs, [sketch])
        tile = zero
        for n, (i, j) in enumerate(own_pairs):
            tile = tile + place(i + 4, j + 4, accs[n])
        for b in range(BLOCKS):
            square = squares[b]
            tile = tile + place(b + 4, 8, square[:, :128] + square[:, 128:])
        local_gram[...] = tile
        pairs = [(i, j) for i in range(BLOCKS) for j in range(i, 2 * BLOCKS)]
        accs = tuple(zero for _ in pairs)
        for c in range(3):
            for k in range(2):
                sketch_wait(c, far_first + k)
                relay_copy(c, far_first + k).start()
            for k in range(2):
                sketch_wait(c, near_first + k)
            store(c).start()
            accs = products(c, accs, pairs, [other, sketch])
        tile = zero
        for n, (i, j) in enumerate(pairs):
            tile = tile + place(i, j, accs[n])
        local_gram[...] += tile

    def sums(first_sem, buffer, me, peer, count):
        return [
            remote(
                buffer.at[me],
                buffer.at[me],
                sum_send.at[first_sem + d],
                sum_recv.at[first_sem + d],
                peer(d + 1),
            )
            for d in range(count - 1)
        ]

    def collect():
        for c in range(3):
            own_copy(c).wait()
            for d in (1, 2, 3):
                sketch_wait(c, lax.rem(in_row + d, 4))
            store(c).start()

    total = local_gram[...]
    levels = [
        (0, row_sums, rank, row_peer, 8),
        (7, plane_sums, gx * 4 + y, plane_peer, 16),
    ]
    for first_sem, buffer, me, peer, count in levels:
        buffer[me] = total
        for copy in sums(first_sem, buffer, me, peer, count):
            copy.start()
        for copy in sums(first_sem, buffer, me, peer, count):
            copy.wait_recv()
        total = buffer[0]
        for k in range(1, count):
            total = total + buffer[k]

    pl.when(sa == 0)(collect)

    gram_out[...] = total

    def drain(merged):
        for e, field in enumerate((field0, field1, field2, field3)):
            for g in range(2):
                for k in range(6):
                    halo_copy(e, g, field, merged, k).wait_send()

    @pl.when(sa == 0)
    def _():
        drain(True)
        for d in (1, 2, 3):
            merge_copy(0, d).wait_send()
        given(0)
        given(1)
        given(2)
        for c in range(3):
            near_copy(c).wait_send()

    @pl.when(sa == 1)
    def _():
        for c in range(3):
            store_own(c).wait()
        drain(False)
        for c in range(3):
            for k in range(2):
                relay_copy(c, far_first + k).wait_send()

    for c in range(3):
        store(c).wait()
    for first_sem, buffer, me, peer, count in levels:
        for copy in sums(first_sem, buffer, me, peer, count):
            copy.wait_send()


def basis_kernel(
    entries, low, high, gram, basis, factor_out, splats, coefs, first, second, result, sems
):
    sa = lax.axis_index("sa")

    def load(c, k):
        src, dst = ((low, first), (high, second))[k]
        return pltpu.make_async_copy(src.at[c], dst.at[c], sems.at[3 * k + c])

    def store(c):
        return pltpu.make_async_copy(result.at[c], basis.at[c], sems.at[6 + c])

    for c in range(3):
        load(c, 0).start()

    @pl.when(sa == 1)
    def _():
        for c in range(3):
            load(c, 1).start()

    total = gram[...]
    row_id = lax.broadcasted_iota(jnp.int32, (8, 128), 0)
    lane_id = lax.broadcasted_iota(jnp.int32, (8, 128), 1)
    for j in range(9):
        turned = total if j == 0 else pltpu.roll(total, 128 - j, 1)
        splats[j] = jnp.broadcast_to(turned[:, 0:1], (8, 128))
    scale = [jnp.sqrt(splats[8, i : i + 1] / entries + 1e-06) for i in range(8)]
    rows = []
    for p in range(8):
        current = {
            j: splats[j, p : p + 1] / entries / (scale[p] * scale[j]) for j in range(p, 8)
        }
        for q in range(p):
            current = {j: current[j] - rows[q][p] * rows[q][j] for j in current}
        root = jnp.sqrt(current[p])
        rows.append({j: current[j] / root for j in current})
    inverse = [None] * 8
    for p in range(7, -1, -1):
        current = {
            j: jnp.full((1, 128), 1.0 if j == p else 0.0, jnp.float32) for j in range(p, 8)
        }
        for q in range(p + 1, 8):
            for j in range(q, 8):
                current[j] = current[j] - rows[p][q] * inverse[q][j]
        inverse[p] = {j: current[j] / rows[p][p] for j in current}
    tile = jnp.zeros((8, 128), jnp.float32)
    for i in range(8):
        for j in range(i, 8):
            tile = tile + jnp.where((row_id == i) & (lane_id == j), rows[i][j], 0.0)
            coefs[i, pl.ds(j, 1)] = inverse[i][j] / scale[i]
    factor_out[...] = tile[:, :8]

    def combine(start, sources):
        weights = {
            (i, j): jnp.broadcast_to(coefs[i, pl.ds(start + j, 1)], (8, 128))
            for j in range(BLOCKS)
            for i in range(start + j + 1)
        }
        for c in range(3):
            for k in range(len(sources)):
                load(c, k).wait()

            def one(x, carry):
                for half in range(2):
                    part = pl.ds(half * 128, 128)
                    values = [s[c, b, x, :, part] for s in sources for b in range(BLOCKS)]
                    for j in range(BLOCKS):
                        acc = weights[0, j] * values[0]
                        for i in range(1, start + j + 1):
                            acc = acc + weights[i, j] * values[i]
                        result[c, j, x, :, part] = acc
                return carry

            lax.fori_loop(0, CELLS, one, 0)
            store(c).start()

    @pl.when(sa == 0)
    def _():
        combine(0, [first])

    @pl.when(sa == 1)
    def _():
        combine(4, [first, second])

    for c in range(3):
        store(c).wait()


def shards(forcing, velocity, wall_solve):
    f32, bf16 = jnp.float32, jnp.bfloat16
    entries = (
        3
        * forcing.shape[2]
        * lax.axis_size("gx")
        * forcing.shape[3]
        * lax.axis_size("gz")
        * forcing.shape[4]
    )
    tile = (3, BLOCKS, CELLS, 8, NY)
    padded = (3, BLOCKS, CELLS + 2, 8, NY)
    edges = (4, 2, 3, BLOCKS, CELLS, 1, NY)
    vmem = pl.BlockSpec(memory_space=pltpu.VMEM)
    hbm = pl.BlockSpec(memory_space=pl.ANY)
    array = jax.ShapeDtypeStruct(tile, f32)
    low, high, gram = pl.pallas_call(
        kernel,
        out_shape=(
            array,
            array,
            jax.ShapeDtypeStruct((8, 128), f32),
        ),
        in_specs=[hbm, vmem, vmem],
        out_specs=(hbm, hbm, vmem),
        scratch_shapes=[
            pltpu.VMEM(padded, f32),
            pltpu.VMEM(padded, f32),
            pltpu.VMEM(padded, f32),
            pltpu.VMEM(padded, f32),
            pltpu.VMEM(tile, f32),
            pltpu.VMEM(tile, f32),
            pltpu.VMEM(tile, f32),
            pltpu.VMEM(edges, f32),
            pltpu.VMEM(edges, f32),
            pltpu.VMEM((PIECE, 3 * NY), bf16),
            pltpu.VMEM((PIECE, 3 * NY), bf16),
            pltpu.VMEM((PIECE, 3 * NY), bf16),
            pltpu.VMEM((PIECE, 3 * NY), bf16),
            pltpu.VMEM((3 * NY, NY), bf16),
            pltpu.VMEM((3 * NY, NY), bf16),
            pltpu.VMEM((1, NY), f32),
            pltpu.VMEM((1, NY), f32),
            pltpu.VMEM((BLOCKS, 8, NY), f32),
            pltpu.VMEM((8, 128), f32),
            pltpu.VMEM((8, 8, 128), f32),
            pltpu.VMEM((16, 8, 128), f32),
            pltpu.SemaphoreType.DMA((2,)),
            pltpu.SemaphoreType.DMA((2, 3)),
            pltpu.SemaphoreType.DMA((2, 3)),
            pltpu.SemaphoreType.DMA((4, 2, 6)),
            pltpu.SemaphoreType.DMA((4, 2, 6)),
            pltpu.SemaphoreType.DMA((3, 4)),
            pltpu.SemaphoreType.DMA((3, 4)),
            pltpu.SemaphoreType.DMA((3, 4)),
            pltpu.SemaphoreType.DMA((3,)),
            pltpu.SemaphoreType.DMA((3,)),
            pltpu.SemaphoreType.DMA((22,)),
            pltpu.SemaphoreType.DMA((22,)),
            pltpu.SemaphoreType.DMA((6,)),
        ],
        compiler_params=pltpu.CompilerParams(
            collective_id=0, has_side_effects=True, vmem_limit_bytes=56 << 20
        ),
        name="sketch",
    )(forcing, velocity.reshape(1, NY), wall_solve)
    return pl.pallas_call(
        functools.partial(basis_kernel, float(entries)),
        out_shape=(array, jax.ShapeDtypeStruct((8, 8), f32)),
        in_specs=[hbm, hbm, vmem],
        out_specs=(hbm, vmem),
        scratch_shapes=[
            pltpu.VMEM((9, 8, 128), f32),
            pltpu.VMEM((8, 8, 128), f32),
            pltpu.VMEM(tile, f32),
            pltpu.VMEM(tile, f32),
            pltpu.VMEM(tile, f32),
            pltpu.SemaphoreType.DMA((9,)),
        ],
        compiler_params=pltpu.CompilerParams(vmem_limit_bytes=60 << 20),
        name="basis",
    )(low, high, gram)


def solution(mesh):
    return jax.shard_map(
        shards,
        mesh=mesh,
        in_specs=(P(None, "sa", "gx", "gz", None), P(), P()),
        out_specs=(P(None, "sa", "gx", "gz", None), P()),
        check_vma=False,
    )
```
